128 devices in a mesh: gx: 16 (over y, x), gz: 8 (over z, core).
Axes of the slice: x: 4, y: 4, z: 4, core: 2. Of those that a mesh axis runs over, the one named last changes fastest.
Arguments:
- populations: float32 [19, 128, 256, 128], P(None, 'gx', 'gz'), may hold values from 0 to 1, as said below
- thermal: float32 [7, 128, 256, 128], P(None, 'gx', 'gz'), may hold values from 0 to 1, as said below
- solid_blocks: float32 [16384, 128], P(('gx', 'gz')), may hold values from 0.05 to 0.95
- centre_dev: int32 [3, 16384, 1], P(None, ('gx', 'gz')), may hold values from 0 to 127; in each aligned block of 128 rows (0 to 127, 128 to 255, ..., all dimensions but the last counted through in order) at most 2 rows name the same one
- centre_col: int32 [3, 16384], P(None, ('gx', 'gz')), may hold values from 0 to 255
- grain_velocity: int32 [3, 3, 16384], P(None, None, ('gx', 'gz')), may hold values from -3200 to 3200
- capture: int32 [3, 16384], P(None, ('gx', 'gz')), may hold values 0 or 1
Outputs:
- flow_out: float32 [19, 128, 256, 128], P(None, 'gx', 'gz')
- heat_out: float32 [7, 128, 256, 128], P(None, 'gx', 'gz')
- solid_out: float32 [16384, 128], P(('gx', 'gz'))
- grain_drag: float32 [3, 16384], P(None, ('gx', 'gz'))
The draws below stay inside these ranges and needn't reach their ends.
Inputs may be any that keep to these rules, and one draw needn't show every extreme that they name: `centre_dev`: in every step the 128 grains held by one device name each device at most 2 times, and some device exactly 2 times. `populations`: every population is positive. `thermal`: every population is positive.
All inputs are finite; a program needn't handle non-finite values. No bound on the sum of `capture` on one device may be relied on, other than what follows from the above.
Results may differ from the reference program's by a relative error of at most 0.0003.
Values sent between devices are 32-bit elements; how exact they have to be, the bound alone decides.
A program may use at most 128 MiB of HBM per device.

```python
import math
import jax
import jax.numpy as jnp
import numpy as np

CX = 8
CZ = 32
CY = 128
G_DEV = 128
STEPS = 3
GRAINS = 16384
CAP = 2
NX = 128
NZ = 256
N_GZ = 8
DEVICES = 128


FLOW_WEIGHTS = [1.0 / 3.0] + [1.0 / 18.0] * 6 + [1.0 / 36.0] * 12


HEAT_WEIGHTS = [0.25] + [0.125] * 6


def draw_populations(key, part):
    key = jax.random.fold_in(key, 5)
    first, second = jax.random.split(key)
    weights = jnp.array(FLOW_WEIGHTS, jnp.float32).reshape(19, 1, 1, 1)
    density = jax.random.uniform(first, (1, NX, NZ, CY), jnp.float32, 0.8, 1.2)
    noise = jax.random.uniform(second, (19, NX, NZ, CY), jnp.float32, -0.2, 0.2)
    return (weights * density * (1.0 + noise)).astype(jnp.float32)


def draw_thermal(key, part):
    key = jax.random.fold_in(key, 9)
    first, second = jax.random.split(key)
    weights = jnp.array(HEAT_WEIGHTS, jnp.float32).reshape(7, 1, 1, 1)
    level = jax.random.uniform(first, (1, NX, NZ, CY), jnp.float32, 0.6, 1.4)
    noise = jax.random.uniform(second, (7, NX, NZ, CY), jnp.float32, -0.2, 0.2)
    return (weights * level * (1.0 + noise)).astype(jnp.float32)


def set_ends(entries, key, low, largest):
    longest = entries.shape.index(max(entries.shape))
    spots = []
    for shift in (0, 1):
        where = [jax.random.randint(jax.random.fold_in(key, axis), (), 0, length) for axis, length in enumerate(entries.shape)]
        where[longest] = (where[longest] + shift) % entries.shape[longest]
        spots.append(tuple(where))
    return entries.at[spots[0]].set(low).at[spots[1]].set(largest)


def steps_of(stream_key, dims, pieces, low, top_value):
    factor_of = 1.0
    for axis_at, shards_of in pieces:
        heights = jax.random.uniform(jax.random.fold_in(jax.random.fold_in(stream_key, 6), axis_at), (shards_of,), jnp.float32, low / len(pieces), top_value / len(pieces))
        factor_of = factor_of * jnp.repeat(jnp.exp(heights), dims[axis_at] // shards_of).reshape((-1,) + (1,) * (len(dims) - 1 - axis_at))
    return factor_of


def shared_out(stream_key, own, number, rows, count, top, limit, slope):
    ranking = jax.random.permutation(stream_key, count)
    crowded, common = load_shares(count, rows * top, limit, slope, True), load_shares(count, rows * top, limit, slope, False)
    places = jnp.arange(count)

    def named(sizes, offset_by):
        used = int((sizes > 0).sum())
        fixed = max(1, used // 4)
        moved = fixed + (places - fixed + offset_by * (used - fixed)) % max(1, count - fixed)
        return jnp.zeros((count,), jnp.int32).at[ranking[jnp.where(places < fixed, places, moved)]].set(jnp.asarray(sizes, jnp.int32))

    sizes = jnp.where(number % 4 == 0, named(crowded, number // 4), named(common, number - number // 4 - 1))
    mixed = jax.random.permutation(jax.random.fold_in(own, 3), count)
    donor, sink = mixed[0:count // 2 * 2:2], mixed[1:count // 2 * 2:2]
    slack = jnp.minimum(sizes[donor] - 1, limit - sizes[sink]) // 2
    slack = jnp.where((donor == ranking[0]) | (sink == ranking[0]) | (sizes[sink] == 0), 0, jnp.maximum(slack, 0))
    moved = jax.random.randint(jax.random.fold_in(own, 4), (count // 2,), 0, 1 << 20) % (slack + 1)
    sizes = sizes.at[donor].add(-moved).at[sink].add(moved)
    labels = jnp.searchsorted(jnp.cumsum(sizes), jnp.arange(rows * top), side="right").astype(jnp.int32)
    listing = labels.reshape(top, rows).T
    listing = listing[jax.random.permutation(jax.random.fold_in(own, 1), rows)]
    offset_by = jax.random.randint(jax.random.fold_in(own, 2), (rows, 1), 0, top)
    return jnp.take_along_axis(listing, (jnp.arange(top)[None, :] + offset_by) % top, axis=1)


def load_shares(amount, total, most, slope, full):
    portions = [(1 << 20) // math.isqrt(grade ** slope) + 1 for grade in range(1, amount + 1)]
    largest = most if full else min(most, max(-(-total // amount), total * portions[0] // sum(portions)))
    least = 1 if total - largest >= amount - 1 else 0
    counts, surplus = [largest] + [least] * (amount - 1), total - largest - least * (amount - 1)
    while surplus > 0:
        free = [i for i in range(1, amount) if counts[i] < largest] or [i for i in range(1, amount) if counts[i] < most]
        pool, left = sum([portions[i] for i in free]), surplus
        for i in free:
            addition = min(most - counts[i], max(1, left * portions[i] // pool), surplus)
            counts[i] = counts[i] + addition
            surplus = surplus - addition
    return np.array(counts)


def setup_inputs(seed: int = 0) -> dict:
    arg_keys = jax.random.split(jax.random.key(seed), 8)
    populations = draw_populations(jax.random.fold_in(arg_keys[7], 71), 0)
    thermal = draw_thermal(jax.random.fold_in(arg_keys[7], 71), 0)
    solid_blocks = jnp.clip(0.05 + 0.9 * jax.random.uniform(arg_keys[2], (GRAINS, CY), jnp.float32) ** steps_of(arg_keys[2], (GRAINS, CY), ((0, 128),), -0.2, 0.2), 0.05, 0.95)
    centre_dev_keys = jax.random.split(jax.random.fold_in(arg_keys[3], 1), STEPS * GRAINS // G_DEV)
    centre_dev_turns = jax.random.permutation(jax.random.fold_in(arg_keys[3], 3), STEPS * GRAINS // G_DEV)
    centre_dev = jax.vmap(lambda own, number: shared_out(jax.random.fold_in(arg_keys[3], 2), own, number, G_DEV, DEVICES, 1, CAP, 2))(centre_dev_keys, centre_dev_turns).reshape((STEPS, GRAINS, 1))
    centre_col = set_ends(jax.random.randint(arg_keys[4], (STEPS, GRAINS), 0, CX * CZ), jax.random.fold_in(arg_keys[4], 1), 0, (CX * CZ) - 1).astype(jnp.int32)
    grain_velocity = set_ends(jax.random.randint(arg_keys[5], (STEPS, 3, GRAINS), -3200, 3201), jax.random.fold_in(arg_keys[5], 1), -3200, 3200).astype(jnp.int32)
    capture = set_ends((jax.random.randint(arg_keys[6], (STEPS, GRAINS), 0, 2) < 1).astype(jnp.int32), jax.random.fold_in(arg_keys[6], 1), 0, 1)
    return dict(populations=populations, thermal=thermal, solid_blocks=solid_blocks, centre_dev=centre_dev, centre_col=centre_col, grain_velocity=grain_velocity, capture=capture)


FLOW = [(0, 0, 0), (1, 0, 0), (-1, 0, 0), (0, 1, 0), (0, -1, 0), (0, 0, 1), (0, 0, -1),
        (1, 1, 0), (-1, -1, 0), (1, -1, 0), (-1, 1, 0), (1, 0, 1), (-1, 0, -1), (1, 0, -1),
        (-1, 0, 1), (0, 1, 1), (0, -1, -1), (0, 1, -1), (0, -1, 1)]
FLOW_WEIGHTS = [1.0 / 3.0] + [1.0 / 18.0] * 6 + [1.0 / 36.0] * 12
HEAT = [(0, 0, 0), (1, 0, 0), (-1, 0, 0), (0, 1, 0), (0, -1, 0), (0, 0, 1), (0, 0, -1)]
HEAT_WEIGHTS = [0.25] + [0.125] * 6
TAU = 0.8
TAU_T = 0.7
BETA = 0.5
BUOY = 0.01
T_LIQ = 1.0
RATE = 1.0
LATENT = 0.5
DRAG_SCALE = 40.0
VEL_UNIT = 1.0 / 32768.0


def dotted(velocity, vector):
    total = 0.0
    for axis_id in range(3):
        if velocity[axis_id] == 1:
            total = total + vector[axis_id]
        elif velocity[axis_id] == -1:
            total = total - vector[axis_id]
    return total


def moments(flow, heat):
    density = flow[0]
    for k in range(1, 19):
        density = density + flow[k]
    speed = []
    for axis_id in range(3):
        moment = 0.0
        for k in range(19):
            if FLOW[k][axis_id] == 1:
                moment = moment + flow[k]
            elif FLOW[k][axis_id] == -1:
                moment = moment - flow[k]
        speed.append(moment / density)
    temper = heat[0]
    for k in range(1, 7):
        temper = temper + heat[k]
    return density, speed, temper


def collide(flow, heat, density, speed, temper, force, latent):
    shifted = [speed[c] + TAU * force[c] / density for c in range(3)]
    square = shifted[0] * shifted[0] + shifted[1] * shifted[1] + shifted[2] * shifted[2]
    posts = []
    for k in range(19):
        along = dotted(FLOW[k], shifted)
        balance = FLOW_WEIGHTS[k] * density * (1.0 + 3.0 * along + 4.5 * along * along - 1.5 * square)
        posts.append(flow[k] + (balance - flow[k]) / TAU)
    for k in range(7):
        along = dotted(HEAT[k], speed)
        balance = HEAT_WEIGHTS[k] * temper * (1.0 + 4.0 * along)
        posts.append(heat[k] + (balance - heat[k]) / TAU_T + HEAT_WEIGHTS[k] * latent)
    return posts


def reference(populations, thermal, solid_blocks, centre_dev, centre_col, grain_velocity, capture):
    flow, heat, solid = populations, thermal, solid_blocks
    drag_total = jnp.zeros((3, GRAINS), jnp.float32)
    for step in range(STEPS):
        density, speed, temper = moments(flow, heat)
        device_id = centre_dev[step, :, 0]
        column = centre_col[step]
        xcell = ((device_id // N_GZ) * CX + column // CZ).astype(jnp.int32)
        zcell = ((device_id % N_GZ) * CZ + column % CZ).astype(jnp.int32)
        velocity = grain_velocity[step].astype(jnp.float32) * VEL_UNIT
        taken = capture[step].astype(jnp.float32)
        blank = jnp.zeros((NX, NZ, CY), jnp.float32)
        cover = blank.at[xcell, zcell].add(solid)
        cover_speed = [blank.at[xcell, zcell].add(solid * velocity[c][:, None]) for c in range(3)]
        temp_at = temper[xcell, zcell]
        drag = [BETA * solid * (speed[c][xcell, zcell] - velocity[c][:, None]) for c in range(3)]
        growth = taken[:, None] * RATE * jnp.maximum(T_LIQ - temp_at, 0.0) * (1.0 - solid)
        latent = blank.at[xcell, zcell].add(growth) * LATENT
        force = [BETA * (cover_speed[c] - cover * speed[c]) for c in range(3)]
        force[2] = force[2] + BUOY * density * (temper - T_LIQ)
        posts = collide(flow, heat, density, speed, temper, force, latent)
        moved = []
        for k, velo in enumerate(FLOW + HEAT):
            moved.append(jnp.roll(posts[k], (velo[0], velo[2], velo[1]), axis=(0, 1, 2)))
        flow = jnp.stack(moved[:19])
        heat = jnp.stack(moved[19:])
        solid = solid + growth
        drag_total = drag_total + DRAG_SCALE * jnp.stack([jnp.mean(d, axis=1) for d in drag])
    return flow, heat, solid, drag_total
```

```python
import functools

import jax
import jax.numpy as jnp
from jax import lax
from jax.experimental import pallas as pl
from jax.experimental.pallas import tpu as pltpu
from jax.sharding import PartitionSpec as P

FLOW = [
    (0, 0, 0), (1, 0, 0), (-1, 0, 0), (0, 1, 0), (0, -1, 0), (0, 0, 1), (0, 0, -1),
    (1, 1, 0), (-1, -1, 0), (1, -1, 0), (-1, 1, 0), (1, 0, 1), (-1, 0, -1), (1, 0, -1),
    (-1, 0, 1), (0, 1, 1), (0, -1, -1), (0, 1, -1), (0, -1, 1),
]
HEAT = [(0, 0, 0), (1, 0, 0), (-1, 0, 0), (0, 1, 0), (0, -1, 0), (0, 0, 1), (0, 0, -1)]
ORDER = [1, 7, 9, 20, 11, 13, 2, 8, 10, 21, 12, 14, 5, 15, 18, 24, 6, 16, 17, 25, 0, 3, 4, 19, 22, 23]
PLACE = [ORDER.index(k) for k in range(26)]
PAIRS = [(1, 2), (3, 4), (5, 6), (7, 8), (9, 10), (11, 12), (13, 14), (15, 16), (17, 18)]
TAU = 0.8
TAU_T = 0.7
BETA = 0.5
BUOY = 0.01
LATENT = 0.5
DRAG_SCALE = 40.0
VEL_UNIT = 1.0 / 32768.0
F32 = jnp.float32
BF16 = jnp.bfloat16
MESH = pl.DeviceIdType.MESH
TOP = 8


def dotted(velocity, vector):
    total = None
    for axis_id in range(3):
        if velocity[axis_id] == 1:
            total = vector[axis_id] if total is None else total + vector[axis_id]
        elif velocity[axis_id] == -1:
            total = -vector[axis_id] if total is None else total - vector[axis_id]
    return total


def halves(block):
    high = block.astype(BF16)
    return high, (block - high.astype(F32)).astype(BF16)


def product(left, right):
    return jnp.dot(left, right, preferred_element_type=F32)


def lanes_of(shape):
    return lax.broadcasted_iota(jnp.int32, shape, 1).astype(F32)


def rows_of(shape):
    return lax.broadcasted_iota(jnp.int32, shape, 0).astype(F32)


def chosen(condition):
    return jnp.where(condition, 1.0, 0.0).astype(F32)


def kernel(
    sizes,
    pop, th, solid_in, cdev, ccol, gvel, cap,
    flow_out, heat_out, solid_out, drag_out,
    w0, w1, w2, w3, dens, speeds, temps, mx_b, speed_b, cover,
    table, pick, pick_t, disp, disp_t, caps, spread, solid, drags, gathered,
    out0_s, out0_r, out1_s, out1_r, out2_s, out2_r,
    back0_s, back0_r, back1_s, back1_r, back2_s, back2_r,
    in_sem, out_sem, halo_ss, halo_rs, grain_ss, grain_rs,
):
    n_gx, n_gz = sizes
    n_dev = n_gx * n_gz
    gx, gz = lax.axis_index("gx"), lax.axis_index("gz")
    me = gx * n_gz + gz
    states = (w0, w1, w2, w3)
    width_x, width_z = dens.shape[0], dens.shape[1]
    grains = solid.shape[0]

    def peers(body):
        def group(i, carry):
            k = 1 + lax.rem(n_gx // 2 + 1 + i, n_gx - 1)
            there = lax.rem(gx + k, n_gx)
            for d in (4, 3, 5, 2, 6, 1, 7, 0):
                body(there, lax.rem(gz + d, n_gz))
            return carry

        lax.fori_loop(0, n_gx - 1, group, 0)
        for d in (4, 3, 5, 2, 6, 1, 7):
            body(gx, lax.rem(gz + d, n_gz))

    barrier = pltpu.get_barrier_semaphore()
    peers(lambda x, z: pl.semaphore_signal(barrier, inc=1, device_id=(x, z), device_id_type=MESH))

    loads = []
    for k in range(26):
        source = pop.at[k] if k < 19 else th.at[k - 19]
        loads.append(
            pltpu.make_async_copy(
                source, w0.at[PLACE[k], pl.ds(1, width_x), pl.ds(TOP, width_z), :], in_sem.at[k]
            )
        )
        loads[-1].start()

    def send_rows(which, source, target):
        def one(x, z):
            pltpu.make_async_remote_copy(
                src_ref=source.at[x * n_gz + z],
                dst_ref=target.at[me],
                send_sem=grain_ss.at[which],
                recv_sem=grain_rs.at[which],
                device_id=(x, z),
                device_id_type=MESH,
            ).start()

        peers(one)
        target[pl.ds(me, 1)] = source[pl.ds(me, 1)]

    def rows_sent(which, source):
        part = source.at[pl.ds(0, n_dev - 1)]
        pltpu.make_async_copy(part, part, grain_ss.at[which]).wait()

    def rows_here(which, target):
        part = target.at[pl.ds(0, n_dev - 1)]
        pltpu.make_async_copy(part, part, grain_rs.at[which]).wait()

    square = (grains, grains)
    lane, row = lanes_of(square), rows_of(square)
    table[...] = jnp.zeros(table.shape, F32)
    for t in range(3):
        table[8 * t : 8 * t + 1, :] = ccol[t : t + 1, :].astype(F32)
        table[8 * t + 1 : 8 * t + 2, :] = cap[t : t + 1, :].astype(F32)
        for c in range(3):
            table[8 * t + 2 + c : 8 * t + 3 + c, :] = gvel[3 * t + c : 3 * t + c + 1, :].astype(F32)
    facts = table[...].T
    facts_moved = pltpu.roll(facts, grains // 2, axis=1)
    details = jnp.zeros((n_dev, grains), F32)
    for t in range(3):
        goal = jnp.broadcast_to(cdev[t : t + 1, :].astype(F32), square)
        goal_t = goal.T
        same = goal == goal_t
        rank = jnp.sum(chosen(same & (row < lane)), axis=0, keepdims=True)
        rank_t = jnp.sum(chosen(same & (lane < row)), axis=1, keepdims=True)
        for s in range(2):
            d = chosen((row == goal) & (rank == s)).astype(BF16)
            d_t = chosen((lane == goal_t) & (rank_t == s)).astype(BF16)
            for half in range(2):
                disp[t, s * n_dev : (s + 1) * n_dev, half * grains : (half + 1) * grains] = d
                at = (2 * half + s) * n_dev
                disp_t[t, :, at : at + n_dev] = d_t
            first = 64 * s + 8 * t
            mine = jnp.where(
                (lane >= first) & (lane < first + 8), facts_moved if s else facts, 0.0
            )
            high, low = halves(mine)
            details = details + product(d, high) + product(d, low)
        caps[t] = jnp.broadcast_to(facts[:, 8 * t + 1 : 8 * t + 2], square)

    def packed(t):
        high, low = halves(solid[...])
        return product(disp[t], jnp.concatenate([high, low], axis=0))

    solid[...] = solid_in[...]
    rows = packed(0)
    out0_s[:, 0, 0:128] = rows[0:n_dev]
    out0_s[:, 0, 128:256] = rows[n_dev : 2 * n_dev]
    out0_s[:, 0, 256:384] = details

    pl.semaphore_wait(barrier, n_dev - 1)
    send_rows(0, out0_s, out0_r)

    def moments(t, x):
        w = states[t]

        def at(k):
            return w[PLACE[k], x + 1, TOP : TOP + width_z, :]

        density = at(0)
        momentum = [None, None, None]
        for a, b in PAIRS:
            one, two = at(a), at(b)
            density = density + (one + two)
            apart = one - two
            for c in range(3):
                if FLOW[a][c] == 1:
                    momentum[c] = apart if momentum[c] is None else momentum[c] + apart
                elif FLOW[a][c] == -1:
                    momentum[c] = momentum[c] - apart
        temper = at(19)
        for k in range(20, 26):
            temper = temper + at(k)
        dens[x] = density
        temps[x] = temper
        inverse = 1.0 / density
        for c in range(3):
            speed = momentum[c] * inverse
            speeds[c, x] = speed
            high, low = halves(speed)
            speed_b[x, :, c * 128 : (c + 1) * 128] = high
            speed_b[width_x + x, :, c * 128 : (c + 1) * 128] = low
        high, low = halves(jnp.maximum(1.0 - temper, 0.0))
        mx_b[x] = high
        mx_b[width_x + x] = low

    def all_moments(t):
        def one(x, carry):
            moments(t, x)
            return carry

        lax.fori_loop(0, width_x, one, 0)

    cells = width_x * width_z

    def make_picks(t):
        detail = out0_r[:, 0, 256:384]
        detail_t = detail.T
        for s in range(2):
            at = 64 * s + 8 * t
            p = chosen(lanes_of((n_dev, cells)) == detail[:, at : at + 1]).astype(BF16)
            p_t = chosen(rows_of((cells, n_dev)) == detail_t[at : at + 1, :]).astype(BF16)
            for half in range(2):
                pick[t, s * n_dev : (s + 1) * n_dev, half * cells : (half + 1) * cells] = p
                k = (2 * half + s) * n_dev
                pick_t[t, :, k : k + n_dev] = p_t

    def gather_mx(t):
        return product(pick[t], mx_b[...].reshape(2 * cells, 128))

    def blocks_here(t, s):
        if t == 0:
            return out0_r[:, 0, s * 128 : (s + 1) * 128]
        return (out1_r if t == 1 else out2_r)[:, s, :]

    def make_cover(t):
        detail = out0_r[:, 0, 256:384]
        for s in range(2):
            block = blocks_here(t, s)
            at = 64 * s + 8 * t
            parts = [block]
            for c in range(3):
                parts.append(block * (detail[:, at + 2 + c : at + 3 + c] * VEL_UNIT))
            parts.append(detail[:, at + 1 : at + 2] * (1.0 - block))
            for c in range(5):
                high, low = halves(parts[c])
                spread[s * n_dev : (s + 1) * n_dev, c * 128 : (c + 1) * 128] = high
                spread[(2 + s) * n_dev : (3 + s) * n_dev, c * 128 : (c + 1) * 128] = low
        cover[...] = product(pick_t[t], spread[...]).reshape(width_x, width_z, 640)

    def gather_speed(t):
        gathered[...] = product(pick[t], speed_b[...].reshape(2 * cells, 384))

    def make_drag(t):
        detail = out0_r[:, 0, 256:384]
        lane_d = lanes_of((n_dev, 128))
        total = drags[...]
        for s in range(2):
            block = blocks_here(t, s)
            at = 64 * s + 8 * t
            for c in range(3):
                speed = gathered[s * n_dev : (s + 1) * n_dev, c * 128 : (c + 1) * 128]
                drag = block * (speed - detail[:, at + 2 + c : at + 3 + c] * VEL_UNIT)
                mean = jnp.sum(drag, axis=1, keepdims=True) * (BETA / 128.0)
                total = jnp.where(lane_d == 8 * (2 * t + s) + c, mean, total)
        drags[...] = total

    def collide(t, x):
        w, after = states[t], states[t + 1]
        tall = 16
        for z in range(0, width_z, tall):
            here = slice(z, z + tall)

            def put(k, value):
                velo = FLOW[k] if k < 19 else HEAT[k - 19]
                if velo[1]:
                    value = pltpu.roll(value, velo[1] % 128, axis=1)
                start = TOP + z + velo[2]
                after[PLACE[k], x + 1 + velo[0], start : start + tall, :] = value

            def at(k):
                return w[PLACE[k], x + 1, TOP + z : TOP + z + tall, :]

            density = dens[x, here, :]
            temper = temps[x, here, :]
            speed = [speeds[c, x, here, :] for c in range(3)]
            spots = [cover[x, here, c * 128 : (c + 1) * 128] for c in range(5)]
            pull = (TAU * BETA) / density
            shifted = [speed[c] + pull * (spots[1 + c] - spots[0] * speed[c]) for c in range(3)]
            shifted[2] = shifted[2] + (TAU * BUOY) * (temper - 1.0)
            square_ = shifted[0] * shifted[0] + shifted[1] * shifted[1] + shifted[2] * shifted[2]
            base18 = density * (1.0 / (18.0 * TAU)) * (1.0 - 1.5 * square_)
            base36 = 0.5 * base18
            way18 = density * (3.0 / (18.0 * TAU))
            way36 = 0.5 * way18
            keep = 1.0 - 1.0 / TAU
            put(0, 6.0 * base18 + keep * at(0))
            for a, b in PAIRS:
                along = dotted(FLOW[a], shifted)
                odd = (way18 if a < 7 else way36) * along
                even = (base18 if a < 7 else base36) + 1.5 * along * odd
                put(a, even + odd + keep * at(a))
                put(b, even - odd + keep * at(b))
            keep = 1.0 - 1.0 / TAU_T
            latent = LATENT * jnp.maximum(1.0 - temper, 0.0) * spots[4]
            warm = temper * (1.0 / TAU_T)
            even = 0.125 * (warm + latent)
            put(19, 2.0 * even + keep * at(19))
            half_warm = 0.5 * warm
            for c, axis_id in ((0, 0), (1, 1), (2, 2)):
                odd = half_warm * speed[axis_id]
                put(20 + 2 * c, even + odd + keep * at(20 + 2 * c))
                put(21 + 2 * c, even - odd + keep * at(21 + 2 * c))

    left, right = lax.rem(gx + n_gx - 1, n_gx), lax.rem(gx + 1, n_gx)
    down, up = lax.rem(gz + n_gz - 1, n_gz), lax.rem(gz + 1, n_gz)
    end_x, end_z = width_x + 1, TOP + width_z
    all_z = pl.ds(TOP, width_z)
    all_x = pl.ds(1, width_x)
    faces_x = [
        (pl.ds(0, 4), end_x, all_z, 1, all_z, (right, gz)),
        (4, end_x, pl.ds(TOP + 1, width_z - 1), 1, pl.ds(TOP + 1, width_z - 1), (right, gz)),
        (5, end_x, pl.ds(TOP, width_z - 1), 1, pl.ds(TOP, width_z - 1), (right, gz)),
        (pl.ds(6, 4), 0, all_z, width_x, all_z, (left, gz)),
        (10, 0, pl.ds(TOP, width_z - 1), width_x, pl.ds(TOP, width_z - 1), (left, gz)),
        (11, 0, pl.ds(TOP + 1, width_z - 1), width_x, pl.ds(TOP + 1, width_z - 1), (left, gz)),
        (4, end_x, pl.ds(end_z, 1), 1, pl.ds(TOP, 1), (right, up)),
        (5, end_x, pl.ds(TOP - 1, 1), 1, pl.ds(end_z - 1, 1), (right, down)),
        (10, 0, pl.ds(TOP - 1, 1), width_x, pl.ds(end_z - 1, 1), (left, down)),
        (11, 0, pl.ds(end_z, 1), width_x, pl.ds(TOP, 1), (left, up)),
    ]
    late_x, early_x = pl.ds(2, width_x - 1), pl.ds(1, width_x - 1)
    faces_z = [
        (pl.ds(12, 4), all_x, pl.ds(end_z, 1), all_x, pl.ds(TOP, 1), (gx, up)),
        (4, late_x, pl.ds(end_z, 1), late_x, pl.ds(TOP, 1), (gx, up)),
        (11, early_x, pl.ds(end_z, 1), early_x, pl.ds(TOP, 1), (gx, up)),
        (pl.ds(16, 4), all_x, pl.ds(TOP - 1, 1), all_x, pl.ds(end_z - 1, 1), (gx, down)),
        (10, early_x, pl.ds(TOP - 1, 1), early_x, pl.ds(end_z - 1, 1), (gx, down)),
        (5, late_x, pl.ds(TOP - 1, 1), late_x, pl.ds(end_z - 1, 1), (gx, down)),
    ]

    def halo(t, which):
        copies = []
        for j, face in enumerate(faces_x + faces_z):
            if (j < len(faces_x)) != (which == 0):
                continue
            k, x_from, z_from, x_to, z_to, to = face
            copies.append(
                pltpu.make_async_remote_copy(
                    src_ref=states[t + 1].at[k, x_from, z_from, :],
                    dst_ref=states[t + 1].at[k, x_to, z_to, :],
                    send_sem=halo_ss.at[16 * t + j],
                    recv_sem=halo_rs.at[16 * t + j],
                    device_id=to,
                    device_id_type=MESH,
                )
            )
        return copies

    def step_flow(t):
        def ends(i, carry):
            collide(t, i * (width_x - 1))
            return carry

        def inner(x, carry):
            collide(t, x)
            return carry

        lax.fori_loop(0, 2, ends, 0)
        first = halo(t, 0)
        for copy in first:
            copy.start()
        lax.fori_loop(1, width_x - 1, inner, 0)
        second = halo(t, 1)
        for copy in second:
            copy.start()
        return first + second

    def grow(t, returned):
        high, low = zip(*[halves(returned(s)) for s in range(2)])
        there = product(disp_t[t], jnp.concatenate(high + low, axis=0))
        now = solid[...]
        solid[...] = now + caps[t] * there * (1.0 - now)

    def pack_rows(t, target):
        rows = packed(t)
        target[:, 0, :] = rows[0:n_dev]
        target[:, 1, :] = rows[n_dev : 2 * n_dev]

    def fill_back(t, target):
        rows = gather_mx(t)
        target[:, 0, :] = rows[0:n_dev]
        target[:, 1, :] = rows[n_dev : 2 * n_dev]

    for copy in loads:
        copy.wait()
    all_moments(0)
    drags[...] = jnp.zeros(drags.shape, F32)
    rows_here(0, out0_r)
    make_picks(0)
    fill_back(0, back0_s)
    send_rows(1, back0_s, back0_r)
    make_cover(0)
    halo0 = step_flow(0)
    gather_speed(0)
    make_drag(0)
    make_picks(1)
    make_picks(2)
    rows_here(1, back0_r)
    grow(0, lambda s: back0_r[:, s, :])
    pack_rows(1, out1_s)
    send_rows(2, out1_s, out1_r)

    for copy in halo0:
        copy.wait_recv()
    all_moments(1)
    fill_back(1, back1_s)
    send_rows(3, back1_s, back1_r)
    gather_speed(1)
    rows_here(2, out1_r)
    make_cover(1)
    halo1 = step_flow(1)
    make_drag(1)
    rows_here(3, back1_r)
    grow(1, lambda s: back1_r[:, s, :])
    pack_rows(2, out2_s)
    send_rows(4, out2_s, out2_r)

    for copy in halo1:
        copy.wait_recv()
    all_moments(2)
    rows = gather_mx(2)
    back2_s[:, 0, 0:128] = rows[0:n_dev]
    back2_s[:, 0, 128:256] = rows[n_dev : 2 * n_dev]
    gather_speed(2)
    rows_here(4, out2_r)
    make_drag(2)
    back2_s[:, 0, 256:384] = drags[...]
    send_rows(5, back2_s, back2_r)
    make_cover(2)
    halo2 = step_flow(2)
    for copy in halo2:
        copy.wait_recv()
    stores = []
    for k in range(26):
        goal = flow_out.at[k] if k < 19 else heat_out.at[k - 19]
        stores.append(
            pltpu.make_async_copy(
                w3.at[PLACE[k], pl.ds(1, width_x), pl.ds(TOP, width_z), :], goal, out_sem.at[k]
            )
        )
        stores[-1].start()
    rows_here(5, back2_r)
    grow(2, lambda s: back2_r[:, 0, s * 128 : (s + 1) * 128])
    solid_out[...] = solid[...]
    means = back2_r[:, 0, 256:384].T
    total = jnp.zeros((8, grains), F32)
    for t in range(3):
        for s in range(2):
            at = 8 * (2 * t + s)
            high, low = halves(means[at : at + 8, :])
            d = disp[t, s * n_dev : (s + 1) * n_dev, 0:grains]
            total = total + product(high, d) + product(low, d)
    drag_out[...] = total[0:3, :] * DRAG_SCALE

    for copy in halo0 + halo1 + halo2:
        copy.wait_send()
    for which, source in enumerate((out0_s, back0_s, out1_s, back1_s, out2_s, back2_s)):
        rows_sent(which, source)
    for copy in stores:
        copy.wait()


def on_device(sizes, populations, thermal, solid_blocks, centre_dev, centre_col, grain_velocity, capture):
    n_dev = sizes[0] * sizes[1]
    width_x, width_z, width_y = populations.shape[1:]
    grains = solid_blocks.shape[0]
    cells = width_x * width_z
    any_ = pl.BlockSpec(memory_space=pl.ANY)
    vmem = pl.BlockSpec(memory_space=pltpu.VMEM)
    state = pltpu.VMEM((26, width_x + 2, width_z + 16, width_y), F32)
    wide = pltpu.VMEM((n_dev, 1, 384), F32)
    plain = pltpu.VMEM((n_dev, 2, 128), F32)
    plane = (width_x, width_z, width_y)
    return pl.pallas_call(
        functools.partial(kernel, sizes),
        out_shape=(
            jax.ShapeDtypeStruct(populations.shape, F32),
            jax.ShapeDtypeStruct(thermal.shape, F32),
            jax.ShapeDtypeStruct(solid_blocks.shape, F32),
            jax.ShapeDtypeStruct((3, grains), F32),
        ),
        in_specs=[any_, any_, vmem, vmem, vmem, vmem, vmem],
        out_specs=(any_, any_, vmem, vmem),
        scratch_shapes=[
            state, state, state, state,
            pltpu.VMEM(plane, F32),
            pltpu.VMEM((3,) + plane, F32),
            pltpu.VMEM(plane, F32),
            pltpu.VMEM((2 * width_x, width_z, 128), BF16),
            pltpu.VMEM((2 * width_x, width_z, 384), BF16),
            pltpu.VMEM((width_x, width_z, 640), F32),
            pltpu.VMEM((128, grains), F32),
            pltpu.VMEM((3, 2 * n_dev, 2 * cells), BF16),
            pltpu.VMEM((3, cells, 4 * n_dev), BF16),
            pltpu.VMEM((3, 2 * n_dev, 2 * grains), BF16),
            pltpu.VMEM((3, grains, 4 * n_dev), BF16),
            pltpu.VMEM((3, grains, 128), F32),
            pltpu.VMEM((4 * n_dev, 640), BF16),
            pltpu.VMEM((grains, 128), F32),
            pltpu.VMEM((n_dev, 128), F32),
            pltpu.VMEM((2 * n_dev, 384), F32),
            wide, wide, plain, plain, plain, plain,
            plain, plain, plain, plain, wide, wide,
            pltpu.SemaphoreType.DMA((26,)),
            pltpu.SemaphoreType.DMA((26,)),
            pltpu.SemaphoreType.DMA((48,)),
            pltpu.SemaphoreType.DMA((48,)),
            pltpu.SemaphoreType.DMA((6,)),
            pltpu.SemaphoreType.DMA((6,)),
        ],
        compiler_params=pltpu.CompilerParams(
            collective_id=0, has_side_effects=True, vmem_limit_bytes=56 * 1024 * 1024
        ),
    )(
        populations,
        thermal,
        solid_blocks,
        centre_dev.reshape(3, grains),
        centre_col,
        grain_velocity.reshape(9, grains),
        capture,
    )


def solution(mesh):
    sizes = (mesh.shape["gx"], mesh.shape["gz"])
    placed = (
        P(None, "gx", "gz", None),
        P(None, "gx", "gz", None),
        P(("gx", "gz"), None),
        P(None, ("gx", "gz"), None),
        P(None, ("gx", "gz")),
        P(None, None, ("gx", "gz")),
        P(None, ("gx", "gz")),
    )
    return jax.shard_map(
        functools.partial(on_device, sizes),
        mesh=mesh,
        in_specs=placed,
        out_specs=(
            P(None, "gx", "gz", None),
            P(None, "gx", "gz", None),
            P(("gx", "gz"), None),
            P(None, ("gx", "gz")),
        ),
        check_vma=False,
    )
```

```python
import functools

import jax
import jax.numpy as jnp
from jax import lax
from jax.experimental import pallas as pl
from jax.experimental.pallas import tpu as pltpu
from jax.sharding import PartitionSpec as P

FLOW = [
    (0, 0, 0), (1, 0, 0), (-1, 0, 0), (0, 1, 0), (0, -1, 0), (0, 0, 1), (0, 0, -1),
    (1, 1, 0), (-1, -1, 0), (1, -1, 0), (-1, 1, 0), (1, 0, 1), (-1, 0, -1), (1, 0, -1),
    (-1, 0, 1), (0, 1, 1), (0, -1, -1), (0, 1, -1), (0, -1, 1),
]
HEAT = [(0, 0, 0), (1, 0, 0), (-1, 0, 0), (0, 1, 0), (0, -1, 0), (0, 0, 1), (0, 0, -1)]
ORDER = [1, 7, 9, 20, 11, 13, 2, 8, 10, 21, 12, 14, 5, 15, 18, 24, 6, 16, 17, 25, 0, 3, 4, 19, 22, 23]
PLACE = [ORDER.index(k) for k in range(26)]
PAIRS = [(1, 2), (3, 4), (5, 6), (7, 8), (9, 10), (11, 12), (13, 14), (15, 16), (17, 18)]
TAU = 0.8
TAU_T = 0.7
BETA = 0.5
BUOY = 0.01
LATENT = 0.5
DRAG_SCALE = 40.0
VEL_UNIT = 1.0 / 32768.0
F32 = jnp.float32
BF16 = jnp.bfloat16
MESH = pl.DeviceIdType.MESH
TOP = 8


def dotted(velocity, vector):
    total = None
    for axis_id in range(3):
        if velocity[axis_id] == 1:
            total = vector[axis_id] if total is None else total + vector[axis_id]
        elif velocity[axis_id] == -1:
            total = -vector[axis_id] if total is None else total - vector[axis_id]
    return total


def halves(block):
    high = block.astype(BF16)
    return high, (block - high.astype(F32)).astype(BF16)


def product(left, right):
    return jnp.dot(left, right, preferred_element_type=F32)


def lanes_of(shape):
    return lax.broadcasted_iota(jnp.int32, shape, 1).astype(F32)


def rows_of(shape):
    return lax.broadcasted_iota(jnp.int32, shape, 0).astype(F32)


def chosen(condition):
    return jnp.where(condition, 1.0, 0.0).astype(F32)


def kernel(
    sizes,
    pop, th, solid_in, cdev_in, ccol_in, gvel_in, cap_in,
    w3, solid_out, drag_out,
    w0, w1, w2, cdev, ccol, gvel, cap, dens, speeds, temps, mx_b, speed_b, cover,
    table, pick, pick_t, disp, disp_t, caps, spread, solid, drags, gathered,
    out0_s, out0_r, out1_s, out1_r, out2_s, out2_r,
    back0_s, back0_r, back1_s, back1_r, back2_s, back2_r, drag_s, drag_r,
    in_sem, halo_ss, halo_rs, grain_ss, grain_rs,
):
    n_gx, n_gz = sizes
    n_dev = n_gx * n_gz
    gx, gz = lax.axis_index("gx"), lax.axis_index("gz")
    me = gx * n_gz + gz
    states = (w0, w1, w2, w3)
    width_x, width_z = dens.shape[0], dens.shape[1]
    grains = solid.shape[0]

    far = n_gx // 4
    at_y = [lax.rem(gx // 4 + d, far) * 4 for d in range(far)]
    at_x = [lax.rem(lax.rem(gx, 4) + d, 4) for d in range(4)]
    at_z = [lax.rem(gz // 2 + d, n_gz // 2) * 2 for d in range(n_gz // 2)]
    at_core = [lax.rem(gz, 2), 1 - lax.rem(gz, 2)]
    by_gx = {(y, x): at_y[y] + at_x[x] for y in range(far) for x in range(4)}
    by_gz = {(z, c): at_z[z] + at_core[c] for z in range(n_gz // 2) for c in range(2)}
    apart = [(a, b) for a in by_gx for b in by_gz][1:]

    def hops(pair):
        (y, x), (z, c) = pair
        return min(y, far - y) + min(x, 4 - x) + min(z, n_gz // 2 - z) + 0.5 * c

    apart.sort(key=hops, reverse=True)

    def peers(body):
        for a, b in apart:
            body(by_gx[a], by_gz[b])

    barrier = pltpu.get_barrier_semaphore()
    peers(lambda x, z: pl.semaphore_signal(barrier, inc=1, device_id=(x, z), device_id_type=MESH))

    loads = []
    for k in range(26):
        source = pop.at[k] if k < 19 else th.at[k - 19]
        loads.append(
            pltpu.make_async_copy(
                source, w0.at[PLACE[k], pl.ds(1, width_x), pl.ds(TOP, width_z), :], in_sem.at[k]
            )
        )
    small = []
    for j, (source, goal) in enumerate(
        ((cdev_in, cdev), (ccol_in, ccol), (gvel_in, gvel), (cap_in, cap), (solid_in, solid))
    ):
        small.append(pltpu.make_async_copy(source, goal, in_sem.at[26 + j]))
    for copy in small + loads:
        copy.start()

    def send_rows(which, source, target):
        def one(x, z):
            pltpu.make_async_remote_copy(
                src_ref=source.at[x * n_gz + z],
                dst_ref=target.at[me],
                send_sem=grain_ss.at[which],
                recv_sem=grain_rs.at[which],
                device_id=(x, z),
                device_id_type=MESH,
            ).start()

        peers(one)
        target[pl.ds(me, 1)] = source[pl.ds(me, 1)]

    def rows_sent(which, source):
        part = source.at[pl.ds(0, n_dev - 1)]
        pltpu.make_async_copy(part, part, grain_ss.at[which]).wait()

    def rows_here(which, target):
        part = target.at[pl.ds(0, n_dev - 1)]
        pltpu.make_async_copy(part, part, grain_rs.at[which]).wait()

    for copy in small:
        copy.wait()
    square = (grains, grains)
    lane, row = lanes_of(square), rows_of(square)
    table[...] = jnp.zeros(table.shape, F32)
    for t in range(3):
        table[8 * t : 8 * t + 1, :] = ccol[t : t + 1, :].astype(F32)
        table[8 * t + 1 : 8 * t + 2, :] = cap[t : t + 1, :].astype(F32)
        for c in range(3):
            table[8 * t + 2 + c : 8 * t + 3 + c, :] = gvel[t, c : c + 1, :].astype(F32)
    facts = table[...].T
    facts_moved = pltpu.roll(facts, grains // 2, axis=1)
    details = jnp.zeros((n_dev, grains), F32)
    for t in range(3):
        goal = jnp.broadcast_to(cdev[t].astype(F32), square)
        goal_t = goal.T
        same = goal == goal_t
        rank = jnp.sum(chosen(same & (row < lane)), axis=0, keepdims=True)
        rank_t = jnp.sum(chosen(same & (lane < row)), axis=1, keepdims=True)
        for s in range(2):
            d = chosen((row == goal) & (rank == s)).astype(BF16)
            d_t = chosen((lane == goal_t) & (rank_t == s)).astype(BF16)
            for half in range(2):
                disp[t, s * n_dev : (s + 1) * n_dev, half * grains : (half + 1) * grains] = d
                at = (2 * half + s) * n_dev
                disp_t[t, :, at : at + n_dev] = d_t
            first = 64 * s + 8 * t
            mine = jnp.where(
                (lane >= first) & (lane < first + 8), facts_moved if s else facts, 0.0
            )
            high, low = halves(mine)
            details = details + product(d, high) + product(d, low)
        caps[t] = jnp.broadcast_to(facts[:, 8 * t + 1 : 8 * t + 2], square)

    def packed(t):
        high, low = halves(solid[...])
        return product(disp[t], jnp.concatenate([high, low], axis=0))

    rows = packed(0)
    out0_s[:, 0, 0:128] = rows[0:n_dev]
    out0_s[:, 0, 128:256] = rows[n_dev : 2 * n_dev]
    out0_s[:, 0, 256:384] = details

    pl.semaphore_wait(barrier, n_dev - 1)
    send_rows(0, out0_s, out0_r)

    def moments(t, x):
        w = states[t]

        def at(k):
            return w[PLACE[k], x + 1, TOP : TOP + width_z, :]

        density = at(0)
        momentum = [None, None, None]
        for a, b in PAIRS:
            one, two = at(a), at(b)
            density = density + (one + two)
            apart = one - two
            for c in range(3):
                if FLOW[a][c] == 1:
                    momentum[c] = apart if momentum[c] is None else momentum[c] + apart
                elif FLOW[a][c] == -1:
                    momentum[c] = momentum[c] - apart
        temper = at(19)
        for k in range(20, 26):
            temper = temper + at(k)
        dens[x] = density
        temps[x] = temper
        inverse = 1.0 / density
        for c in range(3):
            speed = momentum[c] * inverse
            speeds[c, x] = speed
            high, low = halves(speed)
            speed_b[x, :, c * 128 : (c + 1) * 128] = high
            speed_b[width_x + x, :, c * 128 : (c + 1) * 128] = low
        high, low = halves(jnp.maximum(1.0 - temper, 0.0))
        mx_b[x] = high
        mx_b[width_x + x] = low

    def inner_moments(t):
        def one(x, carry):
            moments(t, x)
            return carry

        lax.fori_loop(1, width_x - 1, one, 0)

    def outer_moments(t):
        def one(i, carry):
            moments(t, i * (width_x - 1))
            return carry

        lax.fori_loop(0, 2, one, 0)

    cells = width_x * width_z

    def make_pick(t):
        detail = out0_r[:, 0, 256:384]
        for s in range(2):
            at = 64 * s + 8 * t
            p = chosen(lanes_of((n_dev, cells)) == detail[:, at : at + 1]).astype(BF16)
            for half in range(2):
                pick[t, s * n_dev : (s + 1) * n_dev, half * cells : (half + 1) * cells] = p

    def make_pick_t(t):
        detail_t = out0_r[:, 0, 256:384].T
        for s in range(2):
            at = 64 * s + 8 * t
            p_t = chosen(rows_of((cells, n_dev)) == detail_t[at : at + 1, :]).astype(BF16)
            for half in range(2):
                k = (2 * half + s) * n_dev
                pick_t[t, :, k : k + n_dev] = p_t

    def gather_mx(t):
        return product(pick[t], mx_b[...].reshape(2 * cells, 128))

    def blocks_here(t, s):
        if t == 0:
            return out0_r[:, 0, s * 128 : (s + 1) * 128]
        return (out1_r if t == 1 else out2_r)[:, s, :]

    def make_spread(t):
        detail = out0_r[:, 0, 256:384]
        for s in range(2):
            block = blocks_here(t, s)
            at = 64 * s + 8 * t
            parts = [block]
            for c in range(3):
                parts.append(block * (detail[:, at + 2 + c : at + 3 + c] * VEL_UNIT))
            parts.append(detail[:, at + 1 : at + 2] * (1.0 - block))
            for c in range(5):
                high, low = halves(parts[c])
                spread[s * n_dev : (s + 1) * n_dev, c * 128 : (c + 1) * 128] = high
                spread[(2 + s) * n_dev : (3 + s) * n_dev, c * 128 : (c + 1) * 128] = low

    def outer_cover(t):
        rows = product(
            jnp.concatenate([pick_t[t, 0:width_z], pick_t[t, cells - width_z : cells]], axis=0),
            spread[...],
        )
        cover[0] = rows[0:width_z]
        cover[width_x - 1] = rows[width_z : 2 * width_z]

    def inner_cover(t):
        rows = product(pick_t[t, width_z : cells - width_z], spread[...])
        cover[1 : width_x - 1] = rows.reshape(width_x - 2, width_z, 640)

    def gather_speed(t):
        gathered[...] = product(pick[t], speed_b[...].reshape(2 * cells, 384))

    def make_drag(t):
        detail = out0_r[:, 0, 256:384]
        parts, marks = [], []
        for s in range(2):
            block = blocks_here(t, s)
            at = 64 * s + 8 * t
            for c in range(3):
                speed = gathered[s * n_dev : (s + 1) * n_dev, c * 128 : (c + 1) * 128]
                drag = block * (speed - detail[:, at + 2 + c : at + 3 + c] * VEL_UNIT)
                parts.extend(halves(drag))
                mark = chosen(lanes_of((128, 128)) == 8 * (2 * t + s) + c).astype(BF16)
                marks.extend((mark, mark))
        total = product(jnp.concatenate(parts, axis=1), jnp.concatenate(marks, axis=0))
        drags[...] = drags[...] + total * (BETA / 128.0)

    def collide(t, x):
        w, after = states[t], states[t + 1]
        tall = 16
        for z in range(0, width_z, tall):
            here = slice(z, z + tall)

            def put(k, value):
                velo = FLOW[k] if k < 19 else HEAT[k - 19]
                if velo[1]:
                    value = pltpu.roll(value, velo[1] % 128, axis=1)
                start = TOP + z + velo[2]
                after[PLACE[k], x + 1 + velo[0], start : start + tall, :] = value

            def at(k):
                return w[PLACE[k], x + 1, TOP + z : TOP + z + tall, :]

            density = dens[x, here, :]
            temper = temps[x, here, :]
            speed = [speeds[c, x, here, :] for c in range(3)]
            spots = [cover[x, here, c * 128 : (c + 1) * 128] for c in range(5)]
            pull = (TAU * BETA) / density
            shifted = [speed[c] + pull * (spots[1 + c] - spots[0] * speed[c]) for c in range(3)]
            shifted[2] = shifted[2] + (TAU * BUOY) * (temper - 1.0)
            square_ = shifted[0] * shifted[0] + shifted[1] * shifted[1] + shifted[2] * shifted[2]
            base18 = density * (1.0 / (18.0 * TAU)) * (1.0 - 1.5 * square_)
            base36 = 0.5 * base18
            way18 = density * (3.0 / (18.0 * TAU))
            way36 = 0.5 * way18
            keep = 1.0 - 1.0 / TAU
            put(0, 6.0 * base18 + keep * at(0))
            for a, b in PAIRS:
                along = dotted(FLOW[a], shifted)
                odd = (way18 if a < 7 else way36) * along
                even = (base18 if a < 7 else base36) + 1.5 * along * odd
                put(a, even + odd + keep * at(a))
                put(b, even - odd + keep * at(b))
            keep = 1.0 - 1.0 / TAU_T
            latent = LATENT * jnp.maximum(1.0 - temper, 0.0) * spots[4]
            warm = temper * (1.0 / TAU_T)
            even = 0.125 * (warm + latent)
            put(19, 2.0 * even + keep * at(19))
            half_warm = 0.5 * warm
            for c, axis_id in ((0, 0), (1, 1), (2, 2)):
                odd = half_warm * speed[axis_id]
                put(20 + 2 * c, even + odd + keep * at(20 + 2 * c))
                put(21 + 2 * c, even - odd + keep * at(21 + 2 * c))

    left, right = lax.rem(gx + n_gx - 1, n_gx), lax.rem(gx + 1, n_gx)
    down, up = lax.rem(gz + n_gz - 1, n_gz), lax.rem(gz + 1, n_gz)
    end_x, end_z = width_x + 1, TOP + width_z
    all_z = pl.ds(TOP, width_z)
    all_x = pl.ds(1, width_x)
    faces_x = [
        (pl.ds(0, 4), end_x, all_z, 1, all_z, (right, gz)),
        (4, end_x, pl.ds(TOP + 1, width_z - 1), 1, pl.ds(TOP + 1, width_z - 1), (right, gz)),
        (5, end_x, pl.ds(TOP, width_z - 1), 1, pl.ds(TOP, width_z - 1), (right, gz)),
        (pl.ds(6, 4), 0, all_z, width_x, all_z, (left, gz)),
        (10, 0, pl.ds(TOP, width_z - 1), width_x, pl.ds(TOP, width_z - 1), (left, gz)),
        (11, 0, pl.ds(TOP + 1, width_z - 1), width_x, pl.ds(TOP + 1, width_z - 1), (left, gz)),
        (4, end_x, pl.ds(end_z, 1), 1, pl.ds(TOP, 1), (right, up)),
        (5, end_x, pl.ds(TOP - 1, 1), 1, pl.ds(end_z - 1, 1), (right, down)),
        (10, 0, pl.ds(TOP - 1, 1), width_x, pl.ds(end_z - 1, 1), (left, down)),
        (11, 0, pl.ds(end_z, 1), width_x, pl.ds(TOP, 1), (left, up)),
    ]
    late_x, early_x = pl.ds(2, width_x - 1), pl.ds(1, width_x - 1)
    faces_z = [
        (pl.ds(12, 4), all_x, pl.ds(end_z, 1), all_x, pl.ds(TOP, 1), (gx, up)),
        (4, late_x, pl.ds(end_z, 1), late_x, pl.ds(TOP, 1), (gx, up)),
        (11, early_x, pl.ds(end_z, 1), early_x, pl.ds(TOP, 1), (gx, up)),
        (pl.ds(16, 4), all_x, pl.ds(TOP - 1, 1), all_x, pl.ds(end_z - 1, 1), (gx, down)),
        (10, early_x, pl.ds(TOP - 1, 1), early_x, pl.ds(end_z - 1, 1), (gx, down)),
        (5, late_x, pl.ds(TOP - 1, 1), late_x, pl.ds(end_z - 1, 1), (gx, down)),
    ]

    def halo(t, which):
        copies = []
        for j, face in enumerate(faces_x + faces_z):
            if (j < len(faces_x)) != (which == 0):
                continue
            k, x_from, z_from, x_to, z_to, to = face
            copies.append(
                pltpu.make_async_remote_copy(
                    src_ref=states[t + 1].at[k, x_from, z_from, :],
                    dst_ref=states[t + 1].at[k, x_to, z_to, :],
                    send_sem=halo_ss.at[16 * t + j],
                    recv_sem=halo_rs.at[16 * t + j],
                    device_id=to,
                    device_id_type=MESH,
                )
            )
        return copies

    def outer_flow(t):
        def ends(i, carry):
            collide(t, i * (width_x - 1))
            return carry

        outer_cover(t)
        lax.fori_loop(0, 2, ends, 0)
        copies = halo(t, 0)
        for copy in copies:
            copy.start()
        return copies

    def inner_flow(t):
        def inner(x, carry):
            collide(t, x)
            return carry

        inner_cover(t)
        lax.fori_loop(1, width_x - 1, inner, 0)
        copies = halo(t, 1)
        for copy in copies:
            copy.start()
        return copies

    def grow(t, returned):
        high, low = zip(*[halves(returned(s)) for s in range(2)])
        there = product(disp_t[t], jnp.concatenate(high + low, axis=0))
        now = solid[...]
        solid[...] = now + caps[t] * there * (1.0 - now)

    def pack_rows(t, target):
        rows = packed(t)
        target[:, 0, :] = rows[0:n_dev]
        target[:, 1, :] = rows[n_dev : 2 * n_dev]

    def fill_back(t, target):
        rows = gather_mx(t)
        target[:, 0, :] = rows[0:n_dev]
        target[:, 1, :] = rows[n_dev : 2 * n_dev]

    for copy in loads:
        copy.wait()
    outer_moments(0)
    inner_moments(0)
    drags[...] = jnp.zeros(drags.shape, F32)
    rows_here(0, out0_r)
    make_pick(0)
    fill_back(0, back0_s)
    send_rows(1, back0_s, back0_r)
    make_pick_t(0)
    make_spread(0)
    x0 = outer_flow(0)
    z0 = inner_flow(0)
    make_pick(1)
    make_pick_t(1)
    gather_speed(0)
    make_drag(0)
    make_pick(2)
    make_pick_t(2)
    for copy in z0:
        copy.wait_recv()
    inner_moments(1)
    rows_here(1, back0_r)
    grow(0, lambda s: back0_r[:, s, :])
    pack_rows(1, out1_s)
    send_rows(2, out1_s, out1_r)

    for copy in x0:
        copy.wait_recv()
    outer_moments(1)
    fill_back(1, back1_s)
    send_rows(3, back1_s, back1_r)
    gather_speed(1)
    rows_here(2, out1_r)
    make_spread(1)
    x1 = outer_flow(1)
    rows_here(3, back1_r)
    grow(1, lambda s: back1_r[:, s, :])
    pack_rows(2, out2_s)
    send_rows(4, out2_s, out2_r)
    z1 = inner_flow(1)
    make_drag(1)

    for copy in z1:
        copy.wait_recv()
    inner_moments(2)
    for copy in x1:
        copy.wait_recv()
    outer_moments(2)
    fill_back(2, back2_s)
    send_rows(5, back2_s, back2_r)
    gather_speed(2)
    rows_here(4, out2_r)
    make_drag(2)
    drag_s[:, 0, :] = drags[...]
    send_rows(6, drag_s, drag_r)
    make_spread(2)
    x2 = outer_flow(2)
    z2 = inner_flow(2)
    rows_here(5, back2_r)
    grow(2, lambda s: back2_r[:, s, :])
    solid_out[...] = solid[...]
    rows_here(6, drag_r)
    means = drag_r[:, 0, :].T
    total = jnp.zeros((8, grains), F32)
    for t in range(3):
        for s in range(2):
            at = 8 * (2 * t + s)
            high, low = halves(means[at : at + 8, :])
            d = disp[t, s * n_dev : (s + 1) * n_dev, 0:grains]
            total = total + product(high, d) + product(low, d)
    drag_out[...] = total[0:3, :] * DRAG_SCALE

    for copy in z2 + x2:
        copy.wait_recv()
    for copy in z0 + x0 + z1 + x1 + z2 + x2:
        copy.wait_send()
    sources = (out0_s, back0_s, out1_s, back1_s, out2_s, back2_s, drag_s)
    for which, source in enumerate(sources):
        rows_sent(which, source)


def deliver(state, solid, drag, flow_out, heat_out, solid_out, drag_out, sem):
    width_x, width_z = flow_out.shape[1], flow_out.shape[2]
    copies = [
        pltpu.make_async_copy(solid, solid_out, sem.at[26]),
        pltpu.make_async_copy(drag, drag_out, sem.at[27]),
    ]
    for k in range(26):
        goal = flow_out.at[k] if k < 19 else heat_out.at[k - 19]
        source = state.at[PLACE[k], pl.ds(1, width_x), pl.ds(TOP, width_z), :]
        copies.append(pltpu.make_async_copy(source, goal, sem.at[k]))
    for copy in copies:
        copy.start()
    for copy in copies:
        copy.wait()


def on_device(sizes, populations, thermal, solid_blocks, centre_dev, centre_col, grain_velocity, capture):
    n_dev = sizes[0] * sizes[1]
    width_x, width_z, width_y = populations.shape[1:]
    grains = solid_blocks.shape[0]
    cells = width_x * width_z
    vmem = pl.BlockSpec(memory_space=pltpu.VMEM)
    state = pltpu.VMEM((26, width_x + 2, width_z + 16, width_y), F32)
    wide = pltpu.VMEM((n_dev, 1, 384), F32)
    plain = pltpu.VMEM((n_dev, 2, 128), F32)
    thin = pltpu.VMEM((n_dev, 1, 128), F32)
    plane = (width_x, width_z, width_y)
    hbm = pl.BlockSpec(memory_space=pltpu.HBM)
    operands = (
        populations,
        thermal,
        solid_blocks,
        jnp.swapaxes(centre_dev, 1, 2),
        centre_col,
        grain_velocity,
        capture,
    )
    after, solid, drag = pl.pallas_call(
        functools.partial(kernel, sizes),
        out_shape=(
            state,
            pltpu.VMEM(solid_blocks.shape, F32),
            pltpu.VMEM((3, grains), F32),
        ),
        in_specs=[hbm] * 7,
        out_specs=(vmem, vmem, vmem),
        scratch_shapes=[
            state, state, state,
            pltpu.VMEM((3, 1, grains), jnp.int32),
            pltpu.VMEM((3, grains), jnp.int32),
            pltpu.VMEM((3, 3, grains), jnp.int32),
            pltpu.VMEM((3, grains), jnp.int32),
            pltpu.VMEM(plane, F32),
            pltpu.VMEM((3,) + plane, F32),
            pltpu.VMEM(plane, F32),
            pltpu.VMEM((2 * width_x, width_z, 128), BF16),
            pltpu.VMEM((2 * width_x, width_z, 384), BF16),
            pltpu.VMEM((width_x, width_z, 640), F32),
            pltpu.VMEM((128, grains), F32),
            pltpu.VMEM((3, 2 * n_dev, 2 * cells), BF16),
            pltpu.VMEM((3, cells, 4 * n_dev), BF16),
            pltpu.VMEM((3, 2 * n_dev, 2 * grains), BF16),
            pltpu.VMEM((3, grains, 4 * n_dev), BF16),
            pltpu.VMEM((3, grains, 128), F32),
            pltpu.VMEM((4 * n_dev, 640), BF16),
            pltpu.VMEM((grains, 128), F32),
            pltpu.VMEM((n_dev, 128), F32),
            pltpu.VMEM((2 * n_dev, 384), F32),
            wide, wide, plain, plain, plain, plain,
            plain, plain, plain, plain, plain, plain, thin, thin,
            pltpu.SemaphoreType.DMA((31,)),
            pltpu.SemaphoreType.DMA((48,)),
            pltpu.SemaphoreType.DMA((48,)),
            pltpu.SemaphoreType.DMA((7,)),
            pltpu.SemaphoreType.DMA((7,)),
        ],
        compiler_params=pltpu.CompilerParams(
            collective_id=0, has_side_effects=True, vmem_limit_bytes=50 * 1024 * 1024
        ),
    )(*[pltpu.with_memory_space_constraint(given, pltpu.HBM) for given in operands])
    return pl.pallas_call(
        deliver,
        out_shape=(
            jax.ShapeDtypeStruct(populations.shape, F32),
            jax.ShapeDtypeStruct(thermal.shape, F32),
            jax.ShapeDtypeStruct(solid_blocks.shape, F32),
            jax.ShapeDtypeStruct((3, grains), F32),
        ),
        in_specs=[vmem] * 3,
        out_specs=[hbm] * 4,
        scratch_shapes=[pltpu.SemaphoreType.DMA((28,))],
        compiler_params=pltpu.CompilerParams(vmem_limit_bytes=1024 * 1024),
    )(*[pltpu.with_memory_space_constraint(made, pltpu.VMEM) for made in (after, solid, drag)])


def solution(mesh):
    sizes = (mesh.shape["gx"], mesh.shape["gz"])
    placed = (
        P(None, "gx", "gz", None),
        P(None, "gx", "gz", None),
        P(("gx", "gz"), None),
        P(None, ("gx", "gz"), None),
        P(None, ("gx", "gz")),
        P(None, None, ("gx", "gz")),
        P(None, ("gx", "gz")),
    )
    return jax.shard_map(
        functools.partial(on_device, sizes),
        mesh=mesh,
        in_specs=placed,
        out_specs=(
            P(None, "gx", "gz", None),
            P(None, "gx", "gz", None),
            P(("gx", "gz"), None),
            P(None, ("gx", "gz")),
        ),
        check_vma=False,
    )
```

```python
import functools

import jax
import jax.numpy as jnp
from jax import lax
from jax.experimental import pallas as pl
from jax.experimental.pallas import tpu as pltpu
from jax.sharding import PartitionSpec as P

FLOW = [
    (0, 0, 0), (1, 0, 0), (-1, 0, 0), (0, 1, 0), (0, -1, 0), (0, 0, 1), (0, 0, -1),
    (1, 1, 0), (-1, -1, 0), (1, -1, 0), (-1, 1, 0), (1, 0, 1), (-1, 0, -1), (1, 0, -1),
    (-1, 0, 1), (0, 1, 1), (0, -1, -1), (0, 1, -1), (0, -1, 1),
]
HEAT = [(0, 0, 0), (1, 0, 0), (-1, 0, 0), (0, 1, 0), (0, -1, 0), (0, 0, 1), (0, 0, -1)]
ORDER = [1, 7, 9, 20, 11, 13, 2, 8, 10, 21, 12, 14, 5, 15, 18, 24, 6, 16, 17, 25, 0, 3, 4, 19, 22, 23]
PLACE = [ORDER.index(k) for k in range(26)]
PAIRS = [(1, 2), (3, 4), (5, 6), (7, 8), (9, 10), (11, 12), (13, 14), (15, 16), (17, 18)]
TAU = 0.8
TAU_T = 0.7
BETA = 0.5
BUOY = 0.01
LATENT = 0.5
DRAG_SCALE = 40.0
VEL_UNIT = 1.0 / 32768.0
F32 = jnp.float32
BF16 = jnp.bfloat16
MESH = pl.DeviceIdType.MESH
TOP = 8


def dotted(velocity, vector):
    total = None
    for axis_id in range(3):
        if velocity[axis_id] == 1:
            total = vector[axis_id] if total is None else total + vector[axis_id]
        elif velocity[axis_id] == -1:
            total = -vector[axis_id] if total is None else total - vector[axis_id]
    return total


def halves(block):
    high = block.astype(BF16)
    return high, (block - high.astype(F32)).astype(BF16)


def product(left, right):
    return jnp.dot(left, right, preferred_element_type=F32)


def lanes_of(shape):
    return lax.broadcasted_iota(jnp.int32, shape, 1).astype(F32)


def rows_of(shape):
    return lax.broadcasted_iota(jnp.int32, shape, 0).astype(F32)


def chosen(condition):
    return jnp.where(condition, 1.0, 0.0).astype(F32)


def kernel(
    sizes,
    pop, th, solid_in, cdev_in, ccol_in, gvel_in, cap_in,
    w3, solid_out, drag_out,
    w0, w1, w2, cdev, ccol, gvel, cap, dens, speeds, temps, mx_b, speed_b, cover, warmed,
    table, pick, pick_t, disp, disp_t, caps, fast, taken, spread, spread_h, solid, drags, gathered,
    out0_s, out0_r, out1_s, out1_r, out2_s, out2_r,
    back0_s, back0_r, back1_s, back1_r, back2_s, back2_r,
    in_sem, halo_ss, halo_rs, grain_ss, grain_rs,
):
    n_gx, n_gz = sizes
    n_dev = n_gx * n_gz
    gx, gz = lax.axis_index("gx"), lax.axis_index("gz")
    me = gx * n_gz + gz
    states = (w0, w1, w2, w3)
    width_x, width_z = dens.shape[0], dens.shape[1]
    grains = solid.shape[0]

    far = n_gx // 4
    at_y = [lax.rem(gx // 4 + d, far) * 4 for d in range(far)]
    at_x = [lax.rem(lax.rem(gx, 4) + d, 4) for d in range(4)]
    at_z = [lax.rem(gz // 2 + d, n_gz // 2) * 2 for d in range(n_gz // 2)]
    at_core = [lax.rem(gz, 2), 1 - lax.rem(gz, 2)]
    by_gx = {(y, x): at_y[y] + at_x[x] for y in range(far) for x in range(4)}
    by_gz = {(z, c): at_z[z] + at_core[c] for z in range(n_gz // 2) for c in range(2)}
    apart = [(a, b) for a in by_gx for b in by_gz][1:]

    def hops(pair):
        (y, x), (z, c) = pair
        return min(y, far - y) + min(x, 4 - x) + min(z, n_gz // 2 - z) + 0.5 * c

    apart.sort(key=hops, reverse=True)

    def peers(body):
        for a, b in apart:
            body(by_gx[a], by_gz[b])

    barrier = pltpu.get_barrier_semaphore()
    peers(lambda x, z: pl.semaphore_signal(barrier, inc=1, device_id=(x, z), device_id_type=MESH))

    loads = []
    for k in range(26):
        source = pop.at[k] if k < 19 else th.at[k - 19]
        loads.append(
            pltpu.make_async_copy(
                source, w0.at[PLACE[k], pl.ds(1, width_x), pl.ds(TOP, width_z), :], in_sem.at[k]
            )
        )
    small = []
    for j, (source, goal) in enumerate(
        ((cdev_in, cdev), (ccol_in, ccol), (gvel_in, gvel), (cap_in, cap), (solid_in, solid))
    ):
        small.append(pltpu.make_async_copy(source, goal, in_sem.at[26 + j]))
    for copy in small + loads:
        copy.start()

    def send_rows(which, source, target):
        def one(x, z):
            pltpu.make_async_remote_copy(
                src_ref=source.at[x * n_gz + z],
                dst_ref=target.at[me],
                send_sem=grain_ss.at[which],
                recv_sem=grain_rs.at[which],
                device_id=(x, z),
                device_id_type=MESH,
            ).start()

        peers(one)
        target[pl.ds(me, 1)] = source[pl.ds(me, 1)]

    def rows_sent(which, source):
        part = source.at[pl.ds(0, n_dev - 1)]
        pltpu.make_async_copy(part, part, grain_ss.at[which]).wait()

    def rows_here(which, target):
        part = target.at[pl.ds(0, n_dev - 1)]
        pltpu.make_async_copy(part, part, grain_rs.at[which]).wait()

    for copy in small:
        copy.wait()
    square = (grains, grains)
    lane, row = lanes_of(square), rows_of(square)
    table[...] = jnp.zeros(table.shape, F32)
    for t in range(3):
        table[8 * t : 8 * t + 1, :] = ccol[t : t + 1, :].astype(F32)
        table[8 * t + 1 : 8 * t + 2, :] = cap[t : t + 1, :].astype(F32)
        for c in range(3):
            table[8 * t + 2 + c : 8 * t + 3 + c, :] = gvel[t, c : c + 1, :].astype(F32)
    facts = table[...].T
    facts_moved = pltpu.roll(facts, grains // 2, axis=1)
    details = jnp.zeros((n_dev, grains), F32)
    for t in range(3):
        goal = jnp.broadcast_to(cdev[t].astype(F32), square)
        goal_t = goal.T
        same = goal == goal_t
        rank = jnp.sum(chosen(same & (row < lane)), axis=0, keepdims=True)
        rank_t = jnp.sum(chosen(same & (lane < row)), axis=1, keepdims=True)
        for s in range(2):
            d = chosen((row == goal) & (rank == s)).astype(BF16)
            d_t = chosen((lane == goal_t) & (rank_t == s)).astype(BF16)
            for half in range(2):
                disp[t, s * n_dev : (s + 1) * n_dev, half * grains : (half + 1) * grains] = d
                at = (2 * half + s) * n_dev
                disp_t[t, :, at : at + n_dev] = d_t
            first = 64 * s + 8 * t
            mine = jnp.where(
                (lane >= first) & (lane < first + 8), facts_moved if s else facts, 0.0
            )
            high, low = halves(mine)
            details = details + product(d, high) + product(d, low)
        caps[t] = jnp.broadcast_to(facts[:, 8 * t + 1 : 8 * t + 2], square)

    def packed(t):
        high, low = halves(solid[...])
        return product(disp[t], jnp.concatenate([high, low], axis=0))

    rows = packed(0)
    out0_s[:, 0, 0:128] = rows[0:n_dev]
    out0_s[:, 0, 128:256] = rows[n_dev : 2 * n_dev]
    out0_s[:, 0, 256:384] = details

    pl.semaphore_wait(barrier, n_dev - 1)
    send_rows(0, out0_s, out0_r)

    def flow_moments(t, x):
        w = states[t]

        def at(k):
            return w[PLACE[k], x + 1, TOP : TOP + width_z, :]

        density = at(0)
        momentum = [None, None, None]
        for a, b in PAIRS:
            one, two = at(a), at(b)
            density = density + (one + two)
            apart = one - two
            for c in range(3):
                if FLOW[a][c] == 1:
                    momentum[c] = apart if momentum[c] is None else momentum[c] + apart
                elif FLOW[a][c] == -1:
                    momentum[c] = momentum[c] - apart
        dens[x] = density
        inverse = 1.0 / density
        for c in range(3):
            speed = momentum[c] * inverse
            speeds[c, x] = speed
            high, low = halves(speed)
            speed_b[x, :, c * 128 : (c + 1) * 128] = high
            speed_b[width_x + x, :, c * 128 : (c + 1) * 128] = low

    def heat_moments(t, x):
        w = states[t]
        parts = [w[PLACE[k], x + 1, TOP : TOP + width_z, :] for k in range(19, 26)]
        temper = parts[0]
        for part in parts[1:]:
            temper = temper + part
        temps[t % 2, x] = temper
        high, low = halves(jnp.maximum(1.0 - temper, 0.0))
        mx_b[x] = high
        mx_b[width_x + x] = low

    def over(planes, first, step, body):
        def one(i, carry):
            body(first + i * step)
            return carry

        lax.fori_loop(0, planes, one, 0)

    def inner_moments(t):
        over(width_x - 2, 1, 1, lambda x: flow_moments(t, x))

    def outer_moments(t):
        over(2, 0, width_x - 1, lambda x: flow_moments(t, x))

    def all_heat_moments(t):
        over(width_x, 0, 1, lambda x: heat_moments(t, x))

    cells = width_x * width_z

    def make_pick(t):
        detail = out0_r[:, 0, 256:384]
        for s in range(2):
            at = 64 * s + 8 * t
            p = chosen(lanes_of((n_dev, cells)) == detail[:, at : at + 1]).astype(BF16)
            for half in range(2):
                pick[t, s * n_dev : (s + 1) * n_dev, half * cells : (half + 1) * cells] = p

    def make_pick_t(t):
        detail_t = out0_r[:, 0, 256:384].T
        for s in range(2):
            at = 64 * s + 8 * t
            p_t = chosen(rows_of((cells, n_dev)) == detail_t[at : at + 1, :]).astype(BF16)
            for half in range(2):
                k = (2 * half + s) * n_dev
                pick_t[t, :, k : k + n_dev] = p_t

    def gather_mx(t):
        return product(pick[t], mx_b[...].reshape(2 * cells, 128))

    def blocks_here(t, s):
        if t == 0:
            return out0_r[:, 0, s * 128 : (s + 1) * 128]
        return (out1_r if t == 1 else out2_r)[:, s, :]

    def make_facts(t):
        detail = out0_r[:, 0, 256:384]
        shape = (n_dev, 128)
        for s in range(2):
            at = 64 * s + 8 * t
            taken[t, s] = jnp.broadcast_to(detail[:, at + 1 : at + 2], shape)
            for c in range(3):
                speed = detail[:, at + 2 + c : at + 3 + c] * VEL_UNIT
                fast[t, s, c] = jnp.broadcast_to(speed, shape)

    def make_spread(t):
        for s in range(2):
            block = blocks_here(t, s)
            parts = [block] + [block * fast[t, s, c] for c in range(3)]
            for c in range(4):
                high, low = halves(parts[c])
                spread[s * n_dev : (s + 1) * n_dev, c * 128 : (c + 1) * 128] = high
                spread[(2 + s) * n_dev : (3 + s) * n_dev, c * 128 : (c + 1) * 128] = low

    def heat_cover(t):
        for s in range(2):
            high, low = halves(taken[t, s] * (1.0 - blocks_here(t, s)))
            spread_h[s * n_dev : (s + 1) * n_dev, :] = high
            spread_h[(2 + s) * n_dev : (3 + s) * n_dev, :] = low
        warmed[...] = product(pick_t[t], spread_h[...]).reshape(width_x, width_z, 128)

    def outer_cover(t):
        rows = product(
            jnp.concatenate([pick_t[t, 0:width_z], pick_t[t, cells - width_z : cells]], axis=0),
            spread[...],
        )
        cover[0] = rows[0:width_z]
        cover[width_x - 1] = rows[width_z : 2 * width_z]

    def inner_cover(t):
        rows = product(pick_t[t, width_z : cells - width_z], spread[...])
        cover[1 : width_x - 1] = rows.reshape(width_x - 2, width_z, 512)

    def gather_speed(t):
        gathered[...] = product(pick[t], speed_b[...].reshape(2 * cells, 384))

    def make_drag(t):
        parts, marks = [], []
        for s in range(2):
            block = blocks_here(t, s)
            for c in range(3):
                speed = gathered[s * n_dev : (s + 1) * n_dev, c * 128 : (c + 1) * 128]
                parts.extend(halves(block * (speed - fast[t, s, c])))
                mark = chosen(lanes_of((128, 128)) == 8 * (2 * t + s) + c).astype(BF16)
                marks.extend((mark, mark))
        total = product(jnp.concatenate(parts, axis=1), jnp.concatenate(marks, axis=0))
        drags[...] = drags[...] + total * (BETA / 128.0)

    tall = 16

    def put(t, x, z, k, value):
        velo = FLOW[k] if k < 19 else HEAT[k - 19]
        if velo[1]:
            value = pltpu.roll(value, velo[1] % 128, axis=1)
        start = TOP + z + velo[2]
        states[t + 1][PLACE[k], x + 1 + velo[0], start : start + tall, :] = value

    def at_cell(t, x, z, k):
        return states[t][PLACE[k], x + 1, TOP + z : TOP + z + tall, :]

    def collide_flow(t, x):
        for z in range(0, width_z, tall):
            here = slice(z, z + tall)
            put_, at = functools.partial(put, t, x, z), functools.partial(at_cell, t, x, z)
            density = dens[x, here, :]
            speed = [speeds[c, x, here, :] for c in range(3)]
            spots = [cover[x, here, c * 128 : (c + 1) * 128] for c in range(4)]
            pull = (TAU * BETA) / density
            shifted = [speed[c] + pull * (spots[1 + c] - spots[0] * speed[c]) for c in range(3)]
            shifted[2] = shifted[2] + (TAU * BUOY) * (temps[t % 2, x, here, :] - 1.0)
            square_ = shifted[0] * shifted[0] + shifted[1] * shifted[1] + shifted[2] * shifted[2]
            base18 = density * (1.0 / (18.0 * TAU)) * (1.0 - 1.5 * square_)
            base36 = 0.5 * base18
            way18 = density * (3.0 / (18.0 * TAU))
            way36 = 0.5 * way18
            keep = 1.0 - 1.0 / TAU
            put_(0, 6.0 * base18 + keep * at(0))
            for a, b in PAIRS:
                along = dotted(FLOW[a], shifted)
                odd = (way18 if a < 7 else way36) * along
                even = (base18 if a < 7 else base36) + 1.5 * along * odd
                put_(a, even + odd + keep * at(a))
                put_(b, even - odd + keep * at(b))

    def collide_heat(t, x):
        for z in range(0, width_z, tall):
            here = slice(z, z + tall)
            put_, at = functools.partial(put, t, x, z), functools.partial(at_cell, t, x, z)
            temper = temps[t % 2, x, here, :]
            keep = 1.0 - 1.0 / TAU_T
            latent = LATENT * jnp.maximum(1.0 - temper, 0.0) * warmed[x, here, :]
            warm = temper * (1.0 / TAU_T)
            even = 0.125 * (warm + latent)
            put_(19, 2.0 * even + keep * at(19))
            half_warm = 0.5 * warm
            for c in range(3):
                odd = half_warm * speeds[c, x, here, :]
                put_(20 + 2 * c, even + odd + keep * at(20 + 2 * c))
                put_(21 + 2 * c, even - odd + keep * at(21 + 2 * c))

    left, right = lax.rem(gx + n_gx - 1, n_gx), lax.rem(gx + 1, n_gx)
    down, up = lax.rem(gz + n_gz - 1, n_gz), lax.rem(gz + 1, n_gz)
    end_x, end_z = width_x + 1, TOP + width_z
    all_z = pl.ds(TOP, width_z)
    all_x = pl.ds(1, width_x)
    faces_x = [
        (pl.ds(0, 3), end_x, all_z, 1, all_z, (right, gz)),
        (4, end_x, pl.ds(TOP + 1, width_z - 1), 1, pl.ds(TOP + 1, width_z - 1), (right, gz)),
        (5, end_x, pl.ds(TOP, width_z - 1), 1, pl.ds(TOP, width_z - 1), (right, gz)),
        (pl.ds(6, 3), 0, all_z, width_x, all_z, (left, gz)),
        (10, 0, pl.ds(TOP, width_z - 1), width_x, pl.ds(TOP, width_z - 1), (left, gz)),
        (11, 0, pl.ds(TOP + 1, width_z - 1), width_x, pl.ds(TOP + 1, width_z - 1), (left, gz)),
        (4, end_x, pl.ds(end_z, 1), 1, pl.ds(TOP, 1), (right, up)),
        (5, end_x, pl.ds(TOP - 1, 1), 1, pl.ds(end_z - 1, 1), (right, down)),
        (10, 0, pl.ds(TOP - 1, 1), width_x, pl.ds(end_z - 1, 1), (left, down)),
        (11, 0, pl.ds(end_z, 1), width_x, pl.ds(TOP, 1), (left, up)),
    ]
    late_x, early_x = pl.ds(2, width_x - 1), pl.ds(1, width_x - 1)
    faces_z = [
        (pl.ds(12, 3), all_x, pl.ds(end_z, 1), all_x, pl.ds(TOP, 1), (gx, up)),
        (4, late_x, pl.ds(end_z, 1), late_x, pl.ds(TOP, 1), (gx, up)),
        (11, early_x, pl.ds(end_z, 1), early_x, pl.ds(TOP, 1), (gx, up)),
        (pl.ds(16, 3), all_x, pl.ds(TOP - 1, 1), all_x, pl.ds(end_z - 1, 1), (gx, down)),
        (10, early_x, pl.ds(TOP - 1, 1), early_x, pl.ds(end_z - 1, 1), (gx, down)),
        (5, late_x, pl.ds(TOP - 1, 1), late_x, pl.ds(end_z - 1, 1), (gx, down)),
    ]

    faces_h = [
        (3, end_x, all_z, 1, all_z, (right, gz)),
        (9, 0, all_z, width_x, all_z, (left, gz)),
        (15, all_x, pl.ds(end_z, 1), all_x, pl.ds(TOP, 1), (gx, up)),
        (19, all_x, pl.ds(TOP - 1, 1), all_x, pl.ds(end_z - 1, 1), (gx, down)),
    ]

    def halo(t, first, faces):
        copies = []
        for j, (k, x_from, z_from, x_to, z_to, to) in enumerate(faces):
            copies.append(
                pltpu.make_async_remote_copy(
                    src_ref=states[t + 1].at[k, x_from, z_from, :],
                    dst_ref=states[t + 1].at[k, x_to, z_to, :],
                    send_sem=halo_ss.at[20 * t + first + j],
                    recv_sem=halo_rs.at[20 * t + first + j],
                    device_id=to,
                    device_id_type=MESH,
                )
            )
            copies[-1].start()
        return copies

    def outer_flow(t):
        over(2, 0, width_x - 1, lambda x: collide_flow(t, x))
        return halo(t, 0, faces_x)

    def inner_flow(t):
        over(width_x - 2, 1, 1, lambda x: collide_flow(t, x))
        return halo(t, 10, faces_z)

    def heat(t):
        over(width_x, 0, 1, lambda x: collide_heat(t, x))
        return halo(t, 16, faces_h)

    def landed(copies):
        for copy in copies:
            copy.wait_recv()

    def grow(t, returned):
        high, low = zip(*[halves(returned(s)) for s in range(2)])
        there = product(disp_t[t], jnp.concatenate(high + low, axis=0))
        now = solid[...]
        solid[...] = now + caps[t] * there * (1.0 - now)

    def pack_rows(t, target):
        rows = packed(t)
        target[:, 0, :] = rows[0:n_dev]
        target[:, 1, :] = rows[n_dev : 2 * n_dev]

    def fill_back(t, target):
        rows = gather_mx(t)
        target[:, 0, :] = rows[0:n_dev]
        target[:, 1, :] = rows[n_dev : 2 * n_dev]

    for copy in loads:
        copy.wait()
    outer_moments(0)
    inner_moments(0)
    all_heat_moments(0)
    drags[...] = jnp.zeros(drags.shape, F32)
    rows_here(0, out0_r)
    make_pick(0)
    fill_back(0, back0_s)
    send_rows(1, back0_s, back0_r)
    make_pick_t(0)
    make_facts(0)
    heat_cover(0)
    h0 = heat(0)
    make_spread(0)
    outer_cover(0)
    x0 = outer_flow(0)
    make_pick(1)
    inner_cover(0)
    landed(h0)
    all_heat_moments(1)
    fill_back(1, back1_s)
    send_rows(3, back1_s, back1_r)
    rows_here(1, back0_r)
    grow(0, lambda s: back0_r[:, s, :])
    pack_rows(1, out1_s)
    send_rows(2, out1_s, out1_r)
    z0 = inner_flow(0)
    gather_speed(0)
    make_drag(0)
    make_pick_t(1)
    make_facts(1)
    make_pick(2)
    make_pick_t(2)
    make_facts(2)
    landed(z0)
    inner_moments(1)
    landed(x0)
    outer_moments(1)
    gather_speed(1)

    rows_here(3, back1_r)
    grow(1, lambda s: back1_r[:, s, :])
    pack_rows(2, out2_s)
    send_rows(4, out2_s, out2_r)
    rows_here(2, out1_r)
    make_spread(1)
    outer_cover(1)
    x1 = outer_flow(1)
    heat_cover(1)
    h1 = heat(1)
    inner_cover(1)
    z1 = inner_flow(1)
    make_drag(1)
    rows_here(4, out2_r)
    make_spread(2)
    outer_cover(2)
    inner_cover(2)
    heat_cover(2)

    landed(h1)
    all_heat_moments(2)
    rows = gather_mx(2)
    back2_s[:, 0, 0:128] = rows[0:n_dev]
    back2_s[:, 0, 128:256] = rows[n_dev : 2 * n_dev]
    landed(z1)
    inner_moments(2)
    landed(x1)
    outer_moments(2)
    gather_speed(2)
    make_drag(2)
    back2_s[:, 0, 256:384] = drags[...]
    send_rows(5, back2_s, back2_r)
    x2 = outer_flow(2)
    h2 = heat(2)
    z2 = inner_flow(2)
    rows_here(5, back2_r)
    grow(2, lambda s: back2_r[:, 0, s * 128 : (s + 1) * 128])
    solid_out[...] = solid[...]
    means = back2_r[:, 0, 256:384].T
    total = jnp.zeros((8, grains), F32)
    for t in range(3):
        for s in range(2):
            at = 8 * (2 * t + s)
            high, low = halves(means[at : at + 8, :])
            d = disp[t, s * n_dev : (s + 1) * n_dev, 0:grains]
            total = total + product(high, d) + product(low, d)
    drag_out[...] = total[0:3, :] * DRAG_SCALE

    landed(h2 + z2 + x2)
    for copy in h0 + x0 + z0 + h1 + x1 + z1 + h2 + x2 + z2:
        copy.wait_send()
    sources = (out0_s, back0_s, out1_s, back1_s, out2_s, back2_s)
    for which, source in enumerate(sources):
        rows_sent(which, source)


def deliver(state, solid, drag, flow_out, heat_out, solid_out, drag_out, sem):
    width_x, width_z = flow_out.shape[1], flow_out.shape[2]
    copies = [
        pltpu.make_async_copy(solid, solid_out, sem.at[26]),
        pltpu.make_async_copy(drag, drag_out, sem.at[27]),
    ]
    for k in range(26):
        goal = flow_out.at[k] if k < 19 else heat_out.at[k - 19]
        source = state.at[PLACE[k], pl.ds(1, width_x), pl.ds(TOP, width_z), :]
        copies.append(pltpu.make_async_copy(source, goal, sem.at[k]))
    for copy in copies:
        copy.start()
    for copy in copies:
        copy.wait()


def on_device(sizes, populations, thermal, solid_blocks, centre_dev, centre_col, grain_velocity, capture):
    n_dev = sizes[0] * sizes[1]
    width_x, width_z, width_y = populations.shape[1:]
    grains = solid_blocks.shape[0]
    cells = width_x * width_z
    vmem = pl.BlockSpec(memory_space=pltpu.VMEM)
    state = pltpu.VMEM((26, width_x + 2, width_z + 16, width_y), F32)
    wide = pltpu.VMEM((n_dev, 1, 384), F32)
    plain = pltpu.VMEM((n_dev, 2, 128), F32)
    plane = (width_x, width_z, width_y)
    hbm = pl.BlockSpec(memory_space=pltpu.HBM)
    operands = (
        populations,
        thermal,
        solid_blocks,
        jnp.swapaxes(centre_dev, 1, 2),
        centre_col,
        grain_velocity,
        capture,
    )
    after, solid, drag = pl.pallas_call(
        functools.partial(kernel, sizes),
        out_shape=(
            state,
            pltpu.VMEM(solid_blocks.shape, F32),
            pltpu.VMEM((3, grains), F32),
        ),
        in_specs=[hbm] * 7,
        out_specs=(vmem, vmem, vmem),
        scratch_shapes=[
            state, state, state,
            pltpu.VMEM((3, 1, grains), jnp.int32),
            pltpu.VMEM((3, grains), jnp.int32),
            pltpu.VMEM((3, 3, grains), jnp.int32),
            pltpu.VMEM((3, grains), jnp.int32),
            pltpu.VMEM(plane, F32),
            pltpu.VMEM((3,) + plane, F32),
            pltpu.VMEM((2,) + plane, F32),
            pltpu.VMEM((2 * width_x, width_z, 128), BF16),
            pltpu.VMEM((2 * width_x, width_z, 384), BF16),
            pltpu.VMEM((width_x, width_z, 512), F32),
            pltpu.VMEM(plane, F32),
            pltpu.VMEM((128, grains), F32),
            pltpu.VMEM((3, 2 * n_dev, 2 * cells), BF16),
            pltpu.VMEM((3, cells, 4 * n_dev), BF16),
            pltpu.VMEM((3, 2 * n_dev, 2 * grains), BF16),
            pltpu.VMEM((3, grains, 4 * n_dev), BF16),
            pltpu.VMEM((3, grains, 128), F32),
            pltpu.VMEM((3, 2, 3, n_dev, 128), F32),
            pltpu.VMEM((3, 2, n_dev, 128), F32),
            pltpu.VMEM((4 * n_dev, 512), BF16),
            pltpu.VMEM((4 * n_dev, 128), BF16),
            pltpu.VMEM((grains, 128), F32),
            pltpu.VMEM((n_dev, 128), F32),
            pltpu.VMEM((2 * n_dev, 384), F32),
            wide, wide, plain, plain, plain, plain,
            plain, plain, plain, plain, wide, wide,
            pltpu.SemaphoreType.DMA((31,)),
            pltpu.SemaphoreType.DMA((60,)),
            pltpu.SemaphoreType.DMA((60,)),
            pltpu.SemaphoreType.DMA((6,)),
            pltpu.SemaphoreType.DMA((6,)),
        ],
        compiler_params=pltpu.CompilerParams(
            collective_id=0, has_side_effects=True, vmem_limit_bytes=50 * 1024 * 1024
        ),
    )(*[pltpu.with_memory_space_constraint(given, pltpu.HBM) for given in operands])
    return pl.pallas_call(
        deliver,
        out_shape=(
            jax.ShapeDtypeStruct(populations.shape, F32),
            jax.ShapeDtypeStruct(thermal.shape, F32),
            jax.ShapeDtypeStruct(solid_blocks.shape, F32),
            jax.ShapeDtypeStruct((3, grains), F32),
        ),
        in_specs=[vmem] * 3,
        out_specs=[hbm] * 4,
        scratch_shapes=[pltpu.SemaphoreType.DMA((28,))],
        compiler_params=pltpu.CompilerParams(vmem_limit_bytes=1024 * 1024),
    )(*[pltpu.with_memory_space_constraint(made, pltpu.VMEM) for made in (after, solid, drag)])


def solution(mesh):
    sizes = (mesh.shape["gx"], mesh.shape["gz"])
    placed = (
        P(None, "gx", "gz", None),
        P(None, "gx", "gz", None),
        P(("gx", "gz"), None),
        P(None, ("gx", "gz"), None),
        P(None, ("gx", "gz")),
        P(None, None, ("gx", "gz")),
        P(None, ("gx", "gz")),
    )
    return jax.shard_map(
        functools.partial(on_device, sizes),
        mesh=mesh,
        in_specs=placed,
        out_specs=(
            P(None, "gx", "gz", None),
            P(None, "gx", "gz", None),
            P(("gx", "gz"), None),
            P(None, ("gx", "gz")),
        ),
        check_vma=False,
    )
```

```python
import functools

import jax
import jax.numpy as jnp
from jax import lax
from jax.experimental import pallas as pl
from jax.experimental.pallas import tpu as pltpu
from jax.sharding import PartitionSpec as P

FLOW = [
    (0, 0, 0), (1, 0, 0), (-1, 0, 0), (0, 1, 0), (0, -1, 0), (0, 0, 1), (0, 0, -1),
    (1, 1, 0), (-1, -1, 0), (1, -1, 0), (-1, 1, 0), (1, 0, 1), (-1, 0, -1), (1, 0, -1),
    (-1, 0, 1), (0, 1, 1), (0, -1, -1), (0, 1, -1), (0, -1, 1),
]
HEAT = [(0, 0, 0), (1, 0, 0), (-1, 0, 0), (0, 1, 0), (0, -1, 0), (0, 0, 1), (0, 0, -1)]
ORDER = [1, 7, 9, 20, 11, 13, 2, 8, 10, 21, 12, 14, 5, 15, 18, 24, 6, 16, 17, 25, 0, 3, 4, 19, 22, 23]
PLACE = [ORDER.index(k) for k in range(26)]
PAIRS = [(1, 2), (3, 4), (5, 6), (7, 8), (9, 10), (11, 12), (13, 14), (15, 16), (17, 18)]
TAU = 0.8
TAU_T = 0.7
BETA = 0.5
BUOY = 0.01
LATENT = 0.5
DRAG_SCALE = 40.0
VEL_UNIT = 1.0 / 32768.0
F32 = jnp.float32
BF16 = jnp.bfloat16
MESH = pl.DeviceIdType.MESH
TOP = 8


def dotted(velocity, vector):
    total = None
    for axis_id in range(3):
        if velocity[axis_id] == 1:
            total = vector[axis_id] if total is None else total + vector[axis_id]
        elif velocity[axis_id] == -1:
            total = -vector[axis_id] if total is None else total - vector[axis_id]
    return total


def halves(block):
    high = block.astype(BF16)
    return high, (block - high.astype(F32)).astype(BF16)


def product(left, right):
    return jnp.dot(left, right, preferred_element_type=F32)


def lanes_of(shape):
    return lax.broadcasted_iota(jnp.int32, shape, 1).astype(F32)


def rows_of(shape):
    return lax.broadcasted_iota(jnp.int32, shape, 0).astype(F32)


def chosen(condition):
    return jnp.where(condition, 1.0, 0.0).astype(F32)


def kernel(
    sizes,
    pop, th, solid_in, cdev_in, ccol_in, gvel_in, cap_in,
    w3, solid_out, drag_out,
    w0, w1, w2, cdev, ccol, gvel, cap, dens, speeds, temps, mx_b, speed_b, cover, warmed,
    table, pick, pick_t, disp, disp_t, caps, fast, taken, spread, spread_h, solid, drags, gathered,
    out0_s, out0_r, out1_s, out1_r, out2_s, out2_r,
    back0_s, back0_r, back1_s, back1_r, back2_s, back2_r,
    in_sem, halo_ss, halo_rs, grain_ss, grain_rs,
):
    n_gx, n_gz = sizes
    n_dev = n_gx * n_gz
    gx, gz = lax.axis_index("gx"), lax.axis_index("gz")
    me = gx * n_gz + gz
    states = (w0, w1, w2, w3)
    width_x, width_z = dens.shape[0], dens.shape[1]
    grains = solid.shape[0]

    far = n_gx // 4
    at_y = [lax.rem(gx // 4 + d, far) * 4 for d in range(far)]
    at_x = [lax.rem(lax.rem(gx, 4) + d, 4) for d in range(4)]
    at_z = [lax.rem(gz // 2 + d, n_gz // 2) * 2 for d in range(n_gz // 2)]
    at_core = [lax.rem(gz, 2), 1 - lax.rem(gz, 2)]
    by_gx = {(y, x): at_y[y] + at_x[x] for y in range(far) for x in range(4)}
    by_gz = {(z, c): at_z[z] + at_core[c] for z in range(n_gz // 2) for c in range(2)}
    apart = [(a, b) for a in by_gx for b in by_gz][1:]

    def hops(pair):
        (y, x), (z, c) = pair
        return min(y, far - y) + min(x, 4 - x) + min(z, n_gz // 2 - z) + 0.5 * c

    apart.sort(key=hops, reverse=True)

    def peers(body):
        for a, b in apart:
            body(by_gx[a], by_gz[b])

    barrier = pltpu.get_barrier_semaphore()
    peers(lambda x, z: pl.semaphore_signal(barrier, inc=1, device_id=(x, z), device_id_type=MESH))

    loads = []
    for k in range(26):
        source = pop.at[k] if k < 19 else th.at[k - 19]
        loads.append(
            pltpu.make_async_copy(
                source, w0.at[PLACE[k], pl.ds(1, width_x), pl.ds(TOP, width_z), :], in_sem.at[k]
            )
        )
    small = []
    for j, (source, goal) in enumerate(
        ((cdev_in, cdev), (ccol_in, ccol), (gvel_in, gvel), (cap_in, cap), (solid_in, solid))
    ):
        small.append(pltpu.make_async_copy(source, goal, in_sem.at[26 + j]))
    for copy in small + loads:
        copy.start()

    def send_rows(which, source, target):
        def one(x, z):
            pltpu.make_async_remote_copy(
                src_ref=source.at[x * n_gz + z],
                dst_ref=target.at[me],
                send_sem=grain_ss.at[which],
                recv_sem=grain_rs.at[which],
                device_id=(x, z),
                device_id_type=MESH,
            ).start()

        peers(one)
        target[pl.ds(me, 1)] = source[pl.ds(me, 1)]

    def rows_sent(which, source):
        part = source.at[pl.ds(0, n_dev - 1)]
        pltpu.make_async_copy(part, part, grain_ss.at[which]).wait()

    def rows_here(which, target):
        part = target.at[pl.ds(0, n_dev - 1)]
        pltpu.make_async_copy(part, part, grain_rs.at[which]).wait()

    for copy in small:
        copy.wait()
    square = (grains, grains)
    lane, row = lanes_of(square), rows_of(square)
    table[...] = jnp.zeros(table.shape, F32)
    for t in range(3):
        table[8 * t : 8 * t + 1, :] = ccol[t : t + 1, :].astype(F32)
        table[8 * t + 1 : 8 * t + 2, :] = cap[t : t + 1, :].astype(F32)
        for c in range(3):
            table[8 * t + 2 + c : 8 * t + 3 + c, :] = gvel[t, c : c + 1, :].astype(F32)
    facts = table[...].T
    facts_moved = pltpu.roll(facts, grains // 2, axis=1)
    details = jnp.zeros((n_dev, grains), F32)
    for t in range(3):
        goal = jnp.broadcast_to(cdev[t].astype(F32), square)
        goal_t = goal.T
        same = goal == goal_t
        rank = jnp.sum(chosen(same & (row < lane)), axis=0, keepdims=True)
        rank_t = jnp.sum(chosen(same & (lane < row)), axis=1, keepdims=True)
        for s in range(2):
            d = chosen((row == goal) & (rank == s)).astype(BF16)
            d_t = chosen((lane == goal_t) & (rank_t == s)).astype(BF16)
            for half in range(2):
                disp[t, s * n_dev : (s + 1) * n_dev, half * grains : (half + 1) * grains] = d
                at = (2 * half + s) * n_dev
                disp_t[t, :, at : at + n_dev] = d_t
            first = 64 * s + 8 * t
            mine = jnp.where(
                (lane >= first) & (lane < first + 8), facts_moved if s else facts, 0.0
            )
            high, low = halves(mine)
            details = details + product(d, high) + product(d, low)
        caps[t] = jnp.broadcast_to(facts[:, 8 * t + 1 : 8 * t + 2], square)

    def packed(t):
        high, low = halves(solid[...])
        return product(disp[t], jnp.concatenate([high, low], axis=0))

    rows = packed(0)
    out0_s[:, 0, 0:128] = rows[0:n_dev]
    out0_s[:, 0, 128:256] = rows[n_dev : 2 * n_dev]
    out0_s[:, 0, 256:384] = details

    pl.semaphore_wait(barrier, n_dev - 1)
    send_rows(0, out0_s, out0_r)

    def flow_moments(t, x):
        w = states[t]

        def at(k):
            return w[PLACE[k], x + 1, TOP : TOP + width_z, :]

        density = at(0)
        momentum = [None, None, None]
        for a, b in PAIRS:
            one, two = at(a), at(b)
            density = density + (one + two)
            apart = one - two
            for c in range(3):
                if FLOW[a][c] == 1:
                    momentum[c] = apart if momentum[c] is None else momentum[c] + apart
                elif FLOW[a][c] == -1:
                    momentum[c] = momentum[c] - apart
        dens[x] = density
        inverse = 1.0 / density
        for c in range(3):
            speed = momentum[c] * inverse
            speeds[c, x] = speed
            high, low = halves(speed)
            speed_b[x, :, c * 128 : (c + 1) * 128] = high
            speed_b[width_x + x, :, c * 128 : (c + 1) * 128] = low

    def heat_moments(t, x):
        w = states[t]
        parts = [w[PLACE[k], x + 1, TOP : TOP + width_z, :] for k in range(19, 26)]
        temper = parts[0]
        for part in parts[1:]:
            temper = temper + part
        temps[t % 2, x] = temper
        high, low = halves(jnp.maximum(1.0 - temper, 0.0))
        mx_b[x] = high
        mx_b[width_x + x] = low

    def over(planes, first, step, body):
        def one(i, carry):
            body(first + i * step)
            return carry

        lax.fori_loop(0, planes, one, 0)

    def inner_moments(t):
        over(width_x - 2, 1, 1, lambda x: flow_moments(t, x))

    def outer_moments(t):
        over(2, 0, width_x - 1, lambda x: flow_moments(t, x))

    def all_heat_moments(t):
        over(width_x, 0, 1, lambda x: heat_moments(t, x))

    cells = width_x * width_z

    def make_pick(t):
        detail = out0_r[:, 0, 256:384]
        for s in range(2):
            at = 64 * s + 8 * t
            p = chosen(lanes_of((n_dev, cells)) == detail[:, at : at + 1]).astype(BF16)
            for half in range(2):
                pick[t, s * n_dev : (s + 1) * n_dev, half * cells : (half + 1) * cells] = p

    def make_pick_t(t):
        detail_t = out0_r[:, 0, 256:384].T
        for s in range(2):
            at = 64 * s + 8 * t
            p_t = chosen(rows_of((cells, n_dev)) == detail_t[at : at + 1, :]).astype(BF16)
            for half in range(2):
                k = (2 * half + s) * n_dev
                pick_t[t, :, k : k + n_dev] = p_t

    def gather_mx(t):
        return product(pick[t], mx_b[...].reshape(2 * cells, 128))

    def blocks_here(t, s):
        if t == 0:
            return out0_r[:, 0, s * 128 : (s + 1) * 128]
        return (out1_r if t == 1 else out2_r)[:, s, :]

    def make_facts(t):
        detail = out0_r[:, 0, 256:384]
        shape = (n_dev, 128)
        for s in range(2):
            at = 64 * s + 8 * t
            taken[t, s] = jnp.broadcast_to(detail[:, at + 1 : at + 2], shape)
            for c in range(3):
                speed = detail[:, at + 2 + c : at + 3 + c] * VEL_UNIT
                fast[t, s, c] = jnp.broadcast_to(speed, shape)

    def make_spread(t):
        for s in range(2):
            block = blocks_here(t, s)
            parts = [block] + [block * fast[t, s, c] for c in range(3)]
            for c in range(4):
                high, low = halves(parts[c])
                spread[s * n_dev : (s + 1) * n_dev, c * 128 : (c + 1) * 128] = high
                spread[(2 + s) * n_dev : (3 + s) * n_dev, c * 128 : (c + 1) * 128] = low

    def heat_cover(t):
        for s in range(2):
            high, low = halves(taken[t, s] * (1.0 - blocks_here(t, s)))
            spread_h[s * n_dev : (s + 1) * n_dev, :] = high
            spread_h[(2 + s) * n_dev : (3 + s) * n_dev, :] = low
        warmed[...] = product(pick_t[t], spread_h[...]).reshape(width_x, width_z, 128)

    def outer_cover(t):
        rows = product(
            jnp.concatenate([pick_t[t, 0:width_z], pick_t[t, cells - width_z : cells]], axis=0),
            spread[...],
        )
        cover[0] = rows[0:width_z]
        cover[width_x - 1] = rows[width_z : 2 * width_z]

    def inner_cover(t):
        rows = product(pick_t[t, width_z : cells - width_z], spread[...])
        cover[1 : width_x - 1] = rows.reshape(width_x - 2, width_z, 512)

    def gather_speed(t):
        gathered[...] = product(pick[t], speed_b[...].reshape(2 * cells, 384))

    def make_drag(t):
        parts, marks = [], []
        for s in range(2):
            block = blocks_here(t, s)
            for c in range(3):
                speed = gathered[s * n_dev : (s + 1) * n_dev, c * 128 : (c + 1) * 128]
                parts.extend(halves(block * (speed - fast[t, s, c])))
                mark = chosen(lanes_of((128, 128)) == 8 * (2 * t + s) + c).astype(BF16)
                marks.extend((mark, mark))
        total = product(jnp.concatenate(parts, axis=1), jnp.concatenate(marks, axis=0))
        drags[...] = drags[...] + total * (BETA / 128.0)

    tall = 16

    def put(t, x, z, k, value):
        velo = FLOW[k] if k < 19 else HEAT[k - 19]
        if velo[1]:
            value = pltpu.roll(value, velo[1] % 128, axis=1)
        start = TOP + z + velo[2]
        states[t + 1][PLACE[k], x + 1 + velo[0], start : start + tall, :] = value

    def at_cell(t, x, z, k):
        return states[t][PLACE[k], x + 1, TOP + z : TOP + z + tall, :]

    def collide_flow(t, x):
        for z in range(0, width_z, tall):
            here = slice(z, z + tall)
            put_, at = functools.partial(put, t, x, z), functools.partial(at_cell, t, x, z)
            density = dens[x, here, :]
            speed = [speeds[c, x, here, :] for c in range(3)]
            spots = [cover[x, here, c * 128 : (c + 1) * 128] for c in range(4)]
            pull = (TAU * BETA) / density
            shifted = [speed[c] + pull * (spots[1 + c] - spots[0] * speed[c]) for c in range(3)]
            shifted[2] = shifted[2] + (TAU * BUOY) * (temps[t % 2, x, here, :] - 1.0)
            square_ = shifted[0] * shifted[0] + shifted[1] * shifted[1] + shifted[2] * shifted[2]
            base18 = density * (1.0 / (18.0 * TAU)) * (1.0 - 1.5 * square_)
            base36 = 0.5 * base18
            way18 = density * (3.0 / (18.0 * TAU))
            way36 = 0.5 * way18
            keep = 1.0 - 1.0 / TAU
            put_(0, 6.0 * base18 + keep * at(0))
            for a, b in PAIRS:
                along = dotted(FLOW[a], shifted)
                odd = (way18 if a < 7 else way36) * along
                even = (base18 if a < 7 else base36) + 1.5 * along * odd
                put_(a, even + odd + keep * at(a))
                put_(b, even - odd + keep * at(b))

    def collide_heat(t, x):
        for z in range(0, width_z, tall):
            here = slice(z, z + tall)
            put_, at = functools.partial(put, t, x, z), functools.partial(at_cell, t, x, z)
            temper = temps[t % 2, x, here, :]
            keep = 1.0 - 1.0 / TAU_T
            latent = LATENT * jnp.maximum(1.0 - temper, 0.0) * warmed[x, here, :]
            warm = temper * (1.0 / TAU_T)
            even = 0.125 * (warm + latent)
            put_(19, 2.0 * even + keep * at(19))
            half_warm = 0.5 * warm
            for c in range(3):
                odd = half_warm * speeds[c, x, here, :]
                put_(20 + 2 * c, even + odd + keep * at(20 + 2 * c))
                put_(21 + 2 * c, even - odd + keep * at(21 + 2 * c))

    left, right = lax.rem(gx + n_gx - 1, n_gx), lax.rem(gx + 1, n_gx)
    down, up = lax.rem(gz + n_gz - 1, n_gz), lax.rem(gz + 1, n_gz)
    end_x, end_z = width_x + 1, TOP + width_z
    all_z = pl.ds(TOP, width_z)
    all_x = pl.ds(1, width_x)
    faces_x = [
        (pl.ds(0, 3), end_x, all_z, 1, all_z, (right, gz)),
        (4, end_x, pl.ds(TOP + 1, width_z - 1), 1, pl.ds(TOP + 1, width_z - 1), (right, gz)),
        (5, end_x, pl.ds(TOP, width_z - 1), 1, pl.ds(TOP, width_z - 1), (right, gz)),
        (pl.ds(6, 3), 0, all_z, width_x, all_z, (left, gz)),
        (10, 0, pl.ds(TOP, width_z - 1), width_x, pl.ds(TOP, width_z - 1), (left, gz)),
        (11, 0, pl.ds(TOP + 1, width_z - 1), width_x, pl.ds(TOP + 1, width_z - 1), (left, gz)),
        (4, end_x, pl.ds(end_z, 1), 1, pl.ds(TOP, 1), (right, up)),
        (5, end_x, pl.ds(TOP - 1, 1), 1, pl.ds(end_z - 1, 1), (right, down)),
        (10, 0, pl.ds(TOP - 1, 1), width_x, pl.ds(end_z - 1, 1), (left, down)),
        (11, 0, pl.ds(end_z, 1), width_x, pl.ds(TOP, 1), (left, up)),
    ]
    late_x, early_x = pl.ds(2, width_x - 1), pl.ds(1, width_x - 1)
    faces_z = [
        (pl.ds(12, 3), all_x, pl.ds(end_z, 1), all_x, pl.ds(TOP, 1), (gx, up)),
        (4, late_x, pl.ds(end_z, 1), late_x, pl.ds(TOP, 1), (gx, up)),
        (11, early_x, pl.ds(end_z, 1), early_x, pl.ds(TOP, 1), (gx, up)),
        (pl.ds(16, 3), all_x, pl.ds(TOP - 1, 1), all_x, pl.ds(end_z - 1, 1), (gx, down)),
        (10, early_x, pl.ds(TOP - 1, 1), early_x, pl.ds(end_z - 1, 1), (gx, down)),
        (5, late_x, pl.ds(TOP - 1, 1), late_x, pl.ds(end_z - 1, 1), (gx, down)),
    ]

    faces_h = [
        (3, end_x, all_z, 1, all_z, (right, gz)),
        (9, 0, all_z, width_x, all_z, (left, gz)),
        (15, all_x, pl.ds(end_z, 1), all_x, pl.ds(TOP, 1), (gx, up)),
        (19, all_x, pl.ds(TOP - 1, 1), all_x, pl.ds(end_z - 1, 1), (gx, down)),
    ]

    def halo(t, first, faces):
        copies = []
        for j, (k, x_from, z_from, x_to, z_to, to) in enumerate(faces):
            copies.append(
                pltpu.make_async_remote_copy(
                    src_ref=states[t + 1].at[k, x_from, z_from, :],
                    dst_ref=states[t + 1].at[k, x_to, z_to, :],
                    send_sem=halo_ss.at[20 * t + first + j],
                    recv_sem=halo_rs.at[20 * t + first + j],
                    device_id=to,
                    device_id_type=MESH,
                )
            )
            copies[-1].start()
        return copies

    def outer_flow(t):
        over(2, 0, width_x - 1, lambda x: collide_flow(t, x))
        return halo(t, 0, faces_x)

    def inner_flow(t):
        over(width_x - 2, 1, 1, lambda x: collide_flow(t, x))
        return halo(t, 10, faces_z)

    def heat(t):
        over(width_x, 0, 1, lambda x: collide_heat(t, x))
        return halo(t, 16, faces_h)

    def landed(copies):
        for copy in copies:
            copy.wait_recv()

    def grow(t, returned):
        high, low = zip(*[halves(returned(s)) for s in range(2)])
        there = product(disp_t[t], jnp.concatenate(high + low, axis=0))
        now = solid[...]
        solid[...] = now + caps[t] * there * (1.0 - now)

    def pack_rows(t, target):
        rows = packed(t)
        target[:, 0, :] = rows[0:n_dev]
        target[:, 1, :] = rows[n_dev : 2 * n_dev]

    def fill_back(t, target):
        rows = gather_mx(t)
        target[:, 0, :] = rows[0:n_dev]
        target[:, 1, :] = rows[n_dev : 2 * n_dev]

    for copy in loads:
        copy.wait()
    outer_moments(0)
    inner_moments(0)
    all_heat_moments(0)
    drags[...] = jnp.zeros(drags.shape, F32)
    rows_here(0, out0_r)
    make_pick(0)
    fill_back(0, back0_s)
    send_rows(1, back0_s, back0_r)
    make_pick_t(0)
    make_facts(0)
    heat_cover(0)
    h0 = heat(0)
    make_spread(0)
    outer_cover(0)
    x0 = outer_flow(0)
    make_pick(1)
    inner_cover(0)
    rows_here(1, back0_r)
    grow(0, lambda s: back0_r[:, s, :])
    pack_rows(1, out1_s)
    send_rows(2, out1_s, out1_r)
    landed(h0)
    all_heat_moments(1)
    fill_back(1, back1_s)
    send_rows(3, back1_s, back1_r)
    z0 = inner_flow(0)
    gather_speed(0)
    make_drag(0)
    make_pick_t(1)
    make_facts(1)
    make_pick(2)
    make_pick_t(2)
    make_facts(2)
    landed(z0)
    inner_moments(1)
    landed(x0)
    outer_moments(1)
    gather_speed(1)

    rows_here(2, out1_r)
    make_spread(1)
    outer_cover(1)
    x1 = outer_flow(1)
    rows_here(3, back1_r)
    grow(1, lambda s: back1_r[:, s, :])
    pack_rows(2, out2_s)
    send_rows(4, out2_s, out2_r)
    heat_cover(1)
    h1 = heat(1)
    inner_cover(1)
    z1 = inner_flow(1)
    make_drag(1)

    landed(h1)
    all_heat_moments(2)
    rows = gather_mx(2)
    back2_s[:, 0, 0:128] = rows[0:n_dev]
    back2_s[:, 0, 128:256] = rows[n_dev : 2 * n_dev]
    landed(z1)
    inner_moments(2)
    landed(x1)
    outer_moments(2)
    gather_speed(2)
    rows_here(4, out2_r)
    make_drag(2)
    back2_s[:, 0, 256:384] = drags[...]
    send_rows(5, back2_s, back2_r)
    make_spread(2)
    outer_cover(2)
    x2 = outer_flow(2)
    heat_cover(2)
    h2 = heat(2)
    inner_cover(2)
    z2 = inner_flow(2)
    rows_here(5, back2_r)
    grow(2, lambda s: back2_r[:, 0, s * 128 : (s + 1) * 128])
    solid_out[...] = solid[...]
    means = back2_r[:, 0, 256:384].T
    total = jnp.zeros((8, grains), F32)
    for t in range(3):
        for s in range(2):
            at = 8 * (2 * t + s)
            high, low = halves(means[at : at + 8, :])
            d = disp[t, s * n_dev : (s + 1) * n_dev, 0:grains]
            total = total + product(high, d) + product(low, d)
    drag_out[...] = total[0:3, :] * DRAG_SCALE

    landed(h2 + z2 + x2)
    for copy in h0 + x0 + z0 + h1 + x1 + z1 + h2 + x2 + z2:
        copy.wait_send()
    sources = (out0_s, back0_s, out1_s, back1_s, out2_s, back2_s)
    for which, source in enumerate(sources):
        rows_sent(which, source)


def deliver(state, solid, drag, flow_out, heat_out, solid_out, drag_out, sem):
    width_x, width_z = flow_out.shape[1], flow_out.shape[2]
    copies = [
        pltpu.make_async_copy(solid, solid_out, sem.at[26]),
        pltpu.make_async_copy(drag, drag_out, sem.at[27]),
    ]
    for k in range(26):
        goal = flow_out.at[k] if k < 19 else heat_out.at[k - 19]
        source = state.at[PLACE[k], pl.ds(1, width_x), pl.ds(TOP, width_z), :]
        copies.append(pltpu.make_async_copy(source, goal, sem.at[k]))
    for copy in copies:
        copy.start()
    for copy in copies:
        copy.wait()


def on_device(sizes, populations, thermal, solid_blocks, centre_dev, centre_col, grain_velocity, capture):
    n_dev = sizes[0] * sizes[1]
    width_x, width_z, width_y = populations.shape[1:]
    grains = solid_blocks.shape[0]
    cells = width_x * width_z
    vmem = pl.BlockSpec(memory_space=pltpu.VMEM)
    state = pltpu.VMEM((26, width_x + 2, width_z + 16, width_y), F32)
    wide = pltpu.VMEM((n_dev, 1, 384), F32)
    plain = pltpu.VMEM((n_dev, 2, 128), F32)
    plane = (width_x, width_z, width_y)
    hbm = pl.BlockSpec(memory_space=pltpu.HBM)
    operands = (
        populations,
        thermal,
        solid_blocks,
        jnp.swapaxes(centre_dev, 1, 2),
        centre_col,
        grain_velocity,
        capture,
    )
    after, solid, drag = pl.pallas_call(
        functools.partial(kernel, sizes),
        out_shape=(
            state,
            pltpu.VMEM(solid_blocks.shape, F32),
            pltpu.VMEM((3, grains), F32),
        ),
        in_specs=[hbm] * 7,
        out_specs=(vmem, vmem, vmem),
        scratch_shapes=[
            state, state, state,
            pltpu.VMEM((3, 1, grains), jnp.int32),
            pltpu.VMEM((3, grains), jnp.int32),
            pltpu.VMEM((3, 3, grains), jnp.int32),
            pltpu.VMEM((3, grains), jnp.int32),
            pltpu.VMEM(plane, F32),
            pltpu.VMEM((3,) + plane, F32),
            pltpu.VMEM((2,) + plane, F32),
            pltpu.VMEM((2 * width_x, width_z, 128), BF16),
            pltpu.VMEM((2 * width_x, width_z, 384), BF16),
            pltpu.VMEM((width_x, width_z, 512), F32),
            pltpu.VMEM(plane, F32),
            pltpu.VMEM((128, grains), F32),
            pltpu.VMEM((3, 2 * n_dev, 2 * cells), BF16),
            pltpu.VMEM((3, cells, 4 * n_dev), BF16),
            pltpu.VMEM((3, 2 * n_dev, 2 * grains), BF16),
            pltpu.VMEM((3, grains, 4 * n_dev), BF16),
            pltpu.VMEM((3, grains, 128), F32),
            pltpu.VMEM((3, 2, 3, n_dev, 128), F32),
            pltpu.VMEM((3, 2, n_dev, 128), F32),
            pltpu.VMEM((4 * n_dev, 512), BF16),
            pltpu.VMEM((4 * n_dev, 128), BF16),
            pltpu.VMEM((grains, 128), F32),
            pltpu.VMEM((n_dev, 128), F32),
            pltpu.VMEM((2 * n_dev, 384), F32),
            wide, wide, plain, plain, plain, plain,
            plain, plain, plain, plain, wide, wide,
            pltpu.SemaphoreType.DMA((31,)),
            pltpu.SemaphoreType.DMA((60,)),
            pltpu.SemaphoreType.DMA((60,)),
            pltpu.SemaphoreType.DMA((6,)),
            pltpu.SemaphoreType.DMA((6,)),
        ],
        compiler_params=pltpu.CompilerParams(
            collective_id=0, has_side_effects=True, vmem_limit_bytes=50 * 1024 * 1024
        ),
    )(*[pltpu.with_memory_space_constraint(given, pltpu.HBM) for given in operands])
    return pl.pallas_call(
        deliver,
        out_shape=(
            jax.ShapeDtypeStruct(populations.shape, F32),
            jax.ShapeDtypeStruct(thermal.shape, F32),
            jax.ShapeDtypeStruct(solid_blocks.shape, F32),
            jax.ShapeDtypeStruct((3, grains), F32),
        ),
        in_specs=[vmem] * 3,
        out_specs=[hbm] * 4,
        scratch_shapes=[pltpu.SemaphoreType.DMA((28,))],
        compiler_params=pltpu.CompilerParams(vmem_limit_bytes=1024 * 1024),
    )(*[pltpu.with_memory_space_constraint(made, pltpu.VMEM) for made in (after, solid, drag)])


def solution(mesh):
    sizes = (mesh.shape["gx"], mesh.shape["gz"])
    placed = (
        P(None, "gx", "gz", None),
        P(None, "gx", "gz", None),
        P(("gx", "gz"), None),
        P(None, ("gx", "gz"), None),
        P(None, ("gx", "gz")),
        P(None, None, ("gx", "gz")),
        P(None, ("gx", "gz")),
    )
    return jax.shard_map(
        functools.partial(on_device, sizes),
        mesh=mesh,
        in_specs=placed,
        out_specs=(
            P(None, "gx", "gz", None),
            P(None, "gx", "gz", None),
            P(("gx", "gz"), None),
            P(None, ("gx", "gz")),
        ),
        check_vma=False,
    )
```

```python
import functools

import jax
import jax.numpy as jnp
from jax import lax
from jax.experimental import pallas as pl
from jax.experimental.pallas import tpu as pltpu
from jax.sharding import PartitionSpec as P

FLOW = [
    (0, 0, 0), (1, 0, 0), (-1, 0, 0), (0, 1, 0), (0, -1, 0), (0, 0, 1), (0, 0, -1),
    (1, 1, 0), (-1, -1, 0), (1, -1, 0), (-1, 1, 0), (1, 0, 1), (-1, 0, -1), (1, 0, -1),
    (-1, 0, 1), (0, 1, 1), (0, -1, -1), (0, 1, -1), (0, -1, 1),
]
HEAT = [(0, 0, 0), (1, 0, 0), (-1, 0, 0), (0, 1, 0), (0, -1, 0), (0, 0, 1), (0, 0, -1)]
ORDER = [1, 7, 9, 20, 11, 13, 2, 8, 10, 21, 12, 14, 5, 15, 18, 24, 6, 16, 17, 25, 0, 3, 4, 19, 22, 23]
PLACE = [ORDER.index(k) for k in range(26)]
PAIRS = [(1, 2), (3, 4), (5, 6), (7, 8), (9, 10), (11, 12), (13, 14), (15, 16), (17, 18)]
TAU = 0.8
TAU_T = 0.7
BETA = 0.5
BUOY = 0.01
LATENT = 0.5
DRAG_SCALE = 40.0
VEL_UNIT = 1.0 / 32768.0
F32 = jnp.float32
BF16 = jnp.bfloat16
MESH = pl.DeviceIdType.MESH
TOP = 8


def dotted(velocity, vector):
    total = None
    for axis_id in range(3):
        if velocity[axis_id] == 1:
            total = vector[axis_id] if total is None else total + vector[axis_id]
        elif velocity[axis_id] == -1:
            total = -vector[axis_id] if total is None else total - vector[axis_id]
    return total


def halves(block):
    high = block.astype(BF16)
    return high, (block - high.astype(F32)).astype(BF16)


def product(left, right):
    return jnp.dot(left, right, preferred_element_type=F32)


def lanes_of(shape):
    return lax.broadcasted_iota(jnp.int32, shape, 1).astype(F32)


def rows_of(shape):
    return lax.broadcasted_iota(jnp.int32, shape, 0).astype(F32)


def chosen(condition):
    return jnp.where(condition, 1.0, 0.0).astype(F32)


def kernel(
    sizes,
    pop, th, solid_in, cdev_in, ccol_in, gvel_in, cap_in,
    w3, solid_out, drag_out,
    w0, w1, w2, cdev, ccol, gvel, cap, dens, speeds, temps, mx_b, speed_b, cover, warmed,
    table, pick, pick_t, disp, disp_t, caps, fast, taken, spread, spread_h, solid, drags, gathered,
    out0_s, out0_r, out1_s, out1_r, out2_s, out2_r,
    back0_s, back0_r, back1_s, back1_r, back2_s, back2_r,
    in_sem, halo_ss, halo_rs, grain_ss, grain_rs,
):
    n_gx, n_gz = sizes
    n_dev = n_gx * n_gz
    gx, gz = lax.axis_index("gx"), lax.axis_index("gz")
    me = gx * n_gz + gz
    states = (w0, w1, w2, w3)
    width_x, width_z = dens.shape[0], dens.shape[1]
    grains = solid.shape[0]

    far = n_gx // 4
    at_y = [lax.rem(gx // 4 + d, far) * 4 for d in range(far)]
    at_x = [lax.rem(lax.rem(gx, 4) + d, 4) for d in range(4)]
    at_z = [lax.rem(gz // 2 + d, n_gz // 2) * 2 for d in range(n_gz // 2)]
    at_core = [lax.rem(gz, 2), 1 - lax.rem(gz, 2)]
    by_gx = {(y, x): at_y[y] + at_x[x] for y in range(far) for x in range(4)}
    by_gz = {(z, c): at_z[z] + at_core[c] for z in range(n_gz // 2) for c in range(2)}
    apart = [(a, b) for a in by_gx for b in by_gz][1:]

    def hops(pair):
        (y, x), (z, c) = pair
        return min(y, far - y) + min(x, 4 - x) + min(z, n_gz // 2 - z) + 0.5 * c

    apart.sort(key=hops, reverse=True)

    def peers(body):
        for a, b in apart:
            body(by_gx[a], by_gz[b])

    barrier = pltpu.get_barrier_semaphore()
    peers(lambda x, z: pl.semaphore_signal(barrier, inc=1, device_id=(x, z), device_id_type=MESH))

    loads = []
    for k in range(26):
        source = pop.at[k] if k < 19 else th.at[k - 19]
        loads.append(
            pltpu.make_async_copy(
                source, w0.at[PLACE[k], pl.ds(1, width_x), pl.ds(TOP, width_z), :], in_sem.at[k]
            )
        )
    small = []
    for j, (source, goal) in enumerate(
        ((cdev_in, cdev), (ccol_in, ccol), (gvel_in, gvel), (cap_in, cap), (solid_in, solid))
    ):
        small.append(pltpu.make_async_copy(source, goal, in_sem.at[26 + j]))
    for copy in small + loads:
        copy.start()

    def send_rows(which, source, target):
        def one(x, z):
            pltpu.make_async_remote_copy(
                src_ref=source.at[x * n_gz + z],
                dst_ref=target.at[me],
                send_sem=grain_ss.at[which],
                recv_sem=grain_rs.at[which],
                device_id=(x, z),
                device_id_type=MESH,
            ).start()

        peers(one)
        target[pl.ds(me, 1)] = source[pl.ds(me, 1)]

    def rows_sent(which, source):
        part = source.at[pl.ds(0, n_dev - 1)]
        pltpu.make_async_copy(part, part, grain_ss.at[which]).wait()

    def rows_here(which, target):
        part = target.at[pl.ds(0, n_dev - 1)]
        pltpu.make_async_copy(part, part, grain_rs.at[which]).wait()

    for copy in small:
        copy.wait()
    square = (grains, grains)
    lane, row = lanes_of(square), rows_of(square)
    table[...] = jnp.zeros(table.shape, F32)
    for t in range(3):
        table[8 * t : 8 * t + 1, :] = ccol[t : t + 1, :].astype(F32)
        table[8 * t + 1 : 8 * t + 2, :] = cap[t : t + 1, :].astype(F32)
        for c in range(3):
            table[8 * t + 2 + c : 8 * t + 3 + c, :] = gvel[t, c : c + 1, :].astype(F32)
    facts = table[...].T
    facts_moved = pltpu.roll(facts, grains // 2, axis=1)
    details = jnp.zeros((n_dev, grains), F32)
    for t in range(3):
        goal = jnp.broadcast_to(cdev[t].astype(F32), square)
        goal_t = goal.T
        same = goal == goal_t
        rank = jnp.sum(chosen(same & (row < lane)), axis=0, keepdims=True)
        rank_t = jnp.sum(chosen(same & (lane < row)), axis=1, keepdims=True)
        for s in range(2):
            d = chosen((row == goal) & (rank == s)).astype(BF16)
            d_t = chosen((lane == goal_t) & (rank_t == s)).astype(BF16)
            for half in range(2):
                disp[t, s * n_dev : (s + 1) * n_dev, half * grains : (half + 1) * grains] = d
                at = (2 * half + s) * n_dev
                disp_t[t, :, at : at + n_dev] = d_t
            first = 64 * s + 8 * t
            mine = jnp.where(
                (lane >= first) & (lane < first + 8), facts_moved if s else facts, 0.0
            )
            high, low = halves(mine)
            details = details + product(d, high) + product(d, low)
        caps[t] = jnp.broadcast_to(facts[:, 8 * t + 1 : 8 * t + 2], square)

    def packed(t):
        high, low = halves(solid[...])
        return product(disp[t], jnp.concatenate([high, low], axis=0))

    rows = packed(0)
    out0_s[:, 0, 0:128] = rows[0:n_dev]
    out0_s[:, 0, 128:256] = rows[n_dev : 2 * n_dev]
    out0_s[:, 0, 256:384] = details

    pl.semaphore_wait(barrier, n_dev - 1)
    send_rows(0, out0_s, out0_r)

    def flow_moments(t, x):
        w = states[t]

        def at(k):
            return w[PLACE[k], x + 1, TOP : TOP + width_z, :]

        density = at(0)
        momentum = [None, None, None]
        for a, b in PAIRS:
            one, two = at(a), at(b)
            density = density + (one + two)
            apart = one - two
            for c in range(3):
                if FLOW[a][c] == 1:
                    momentum[c] = apart if momentum[c] is None else momentum[c] + apart
                elif FLOW[a][c] == -1:
                    momentum[c] = momentum[c] - apart
        dens[x] = density
        inverse = 1.0 / density
        for c in range(3):
            speed = momentum[c] * inverse
            speeds[c, x] = speed
            high, low = halves(speed)
            speed_b[x, :, c * 128 : (c + 1) * 128] = high
            speed_b[width_x + x, :, c * 128 : (c + 1) * 128] = low

    def heat_moments(t, x):
        w = states[t]
        parts = [w[PLACE[k], x + 1, TOP : TOP + width_z, :] for k in range(19, 26)]
        temper = parts[0]
        for part in parts[1:]:
            temper = temper + part
        temps[t % 2, x] = temper
        high, low = halves(jnp.maximum(1.0 - temper, 0.0))
        mx_b[x] = high
        mx_b[width_x + x] = low

    def over(planes, first, step, body):
        def one(i, carry):
            body(first + i * step)
            return carry

        lax.fori_loop(0, planes, one, 0)

    def inner_moments(t):
        over(width_x - 2, 1, 1, lambda x: flow_moments(t, x))

    def outer_moments(t):
        over(2, 0, width_x - 1, lambda x: flow_moments(t, x))

    def all_heat_moments(t):
        over(width_x, 0, 1, lambda x: heat_moments(t, x))

    cells = width_x * width_z

    def make_pick(t):
        detail = out0_r[:, 0, 256:384]
        for s in range(2):
            at = 64 * s + 8 * t
            p = chosen(lanes_of((n_dev, cells)) == detail[:, at : at + 1]).astype(BF16)
            for half in range(2):
                pick[t, s * n_dev : (s + 1) * n_dev, half * cells : (half + 1) * cells] = p

    def make_pick_t(t):
        detail_t = out0_r[:, 0, 256:384].T
        for s in range(2):
            at = 64 * s + 8 * t
            p_t = chosen(rows_of((cells, n_dev)) == detail_t[at : at + 1, :]).astype(BF16)
            for half in range(2):
                k = (2 * half + s) * n_dev
                pick_t[t, :, k : k + n_dev] = p_t

    def gather_mx(t):
        return product(pick[t], mx_b[...].reshape(2 * cells, 128))

    def blocks_here(t, s):
        if t == 0:
            return out0_r[:, 0, s * 128 : (s + 1) * 128]
        return (out1_r if t == 1 else out2_r)[:, s, :]

    def make_facts(t):
        detail = out0_r[:, 0, 256:384]
        shape = (n_dev, 128)
        for s in range(2):
            at = 64 * s + 8 * t
            taken[t, s] = jnp.broadcast_to(detail[:, at + 1 : at + 2], shape)
            for c in range(3):
                speed = detail[:, at + 2 + c : at + 3 + c] * VEL_UNIT
                fast[t, s, c] = jnp.broadcast_to(speed, shape)

    def make_spread(t):
        for s in range(2):
            block = blocks_here(t, s)
            parts = [block] + [block * fast[t, s, c] for c in range(3)]
            for c in range(4):
                high, low = halves(parts[c])
                spread[s * n_dev : (s + 1) * n_dev, c * 128 : (c + 1) * 128] = high
                spread[(2 + s) * n_dev : (3 + s) * n_dev, c * 128 : (c + 1) * 128] = low

    def heat_cover(t):
        for s in range(2):
            high, low = halves(taken[t, s] * (1.0 - blocks_here(t, s)))
            spread_h[s * n_dev : (s + 1) * n_dev, :] = high
            spread_h[(2 + s) * n_dev : (3 + s) * n_dev, :] = low
        warmed[...] = product(pick_t[t], spread_h[...]).reshape(width_x, width_z, 128)

    def outer_cover(t):
        rows = product(
            jnp.concatenate([pick_t[t, 0:width_z], pick_t[t, cells - width_z : cells]], axis=0),
            spread[...],
        )
        cover[0] = rows[0:width_z]
        cover[width_x - 1] = rows[width_z : 2 * width_z]

    def inner_cover(t):
        rows = product(pick_t[t, width_z : cells - width_z], spread[...])
        cover[1 : width_x - 1] = rows.reshape(width_x - 2, width_z, 512)

    def gather_speed(t):
        gathered[...] = product(pick[t], speed_b[...].reshape(2 * cells, 384))

    def make_drag(t):
        parts, marks = [], []
        for s in range(2):
            block = blocks_here(t, s)
            for c in range(3):
                speed = gathered[s * n_dev : (s + 1) * n_dev, c * 128 : (c + 1) * 128]
                parts.extend(halves(block * (speed - fast[t, s, c])))
                mark = chosen(lanes_of((128, 128)) == 8 * (2 * t + s) + c).astype(BF16)
                marks.extend((mark, mark))
        total = product(jnp.concatenate(parts, axis=1), jnp.concatenate(marks, axis=0))
        drags[...] = drags[...] + total * (BETA / 128.0)

    tall = 16

    def put(t, x, z, k, value):
        velo = FLOW[k] if k < 19 else HEAT[k - 19]
        if velo[1]:
            value = pltpu.roll(value, velo[1] % 128, axis=1)
        start = TOP + z + velo[2]
        states[t + 1][PLACE[k], x + 1 + velo[0], start : start + tall, :] = value

    def at_cell(t, x, z, k):
        return states[t][PLACE[k], x + 1, TOP + z : TOP + z + tall, :]

    def collide_flow(t, x):
        for z in range(0, width_z, tall):
            here = slice(z, z + tall)
            put_, at = functools.partial(put, t, x, z), functools.partial(at_cell, t, x, z)
            density = dens[x, here, :]
            speed = [speeds[c, x, here, :] for c in range(3)]
            spots = [cover[x, here, c * 128 : (c + 1) * 128] for c in range(4)]
            pull = (TAU * BETA) / density
            shifted = [speed[c] + pull * (spots[1 + c] - spots[0] * speed[c]) for c in range(3)]
            shifted[2] = shifted[2] + (TAU * BUOY) * (temps[t % 2, x, here, :] - 1.0)
            square_ = shifted[0] * shifted[0] + shifted[1] * shifted[1] + shifted[2] * shifted[2]
            base18 = density * (1.0 / (18.0 * TAU)) * (1.0 - 1.5 * square_)
            base36 = 0.5 * base18
            way18 = density * (3.0 / (18.0 * TAU))
            way36 = 0.5 * way18
            keep = 1.0 - 1.0 / TAU
            put_(0, 6.0 * base18 + keep * at(0))
            for a, b in PAIRS:
                along = dotted(FLOW[a], shifted)
                odd = (way18 if a < 7 else way36) * along
                even = (base18 if a < 7 else base36) + 1.5 * along * odd
                put_(a, even + odd + keep * at(a))
                put_(b, even - odd + keep * at(b))

    def collide_heat(t, x):
        for z in range(0, width_z, tall):
            here = slice(z, z + tall)
            put_, at = functools.partial(put, t, x, z), functools.partial(at_cell, t, x, z)
            temper = temps[t % 2, x, here, :]
            keep = 1.0 - 1.0 / TAU_T
            latent = LATENT * jnp.maximum(1.0 - temper, 0.0) * warmed[x, here, :]
            warm = temper * (1.0 / TAU_T)
            even = 0.125 * (warm + latent)
            put_(19, 2.0 * even + keep * at(19))
            half_warm = 0.5 * warm
            for c in range(3):
                odd = half_warm * speeds[c, x, here, :]
                put_(20 + 2 * c, even + odd + keep * at(20 + 2 * c))
                put_(21 + 2 * c, even - odd + keep * at(21 + 2 * c))

    left, right = lax.rem(gx + n_gx - 1, n_gx), lax.rem(gx + 1, n_gx)
    down, up = lax.rem(gz + n_gz - 1, n_gz), lax.rem(gz + 1, n_gz)
    end_x, end_z = width_x + 1, TOP + width_z
    all_z = pl.ds(TOP, width_z)
    all_x = pl.ds(1, width_x)
    faces_x = [
        (pl.ds(0, 3), end_x, all_z, 1, all_z, (right, gz)),
        (4, end_x, pl.ds(TOP + 1, width_z - 1), 1, pl.ds(TOP + 1, width_z - 1), (right, gz)),
        (5, end_x, pl.ds(TOP, width_z - 1), 1, pl.ds(TOP, width_z - 1), (right, gz)),
        (pl.ds(6, 3), 0, all_z, width_x, all_z, (left, gz)),
        (10, 0, pl.ds(TOP, width_z - 1), width_x, pl.ds(TOP, width_z - 1), (left, gz)),
        (11, 0, pl.ds(TOP + 1, width_z - 1), width_x, pl.ds(TOP + 1, width_z - 1), (left, gz)),
        (4, end_x, pl.ds(end_z, 1), 1, pl.ds(TOP, 1), (right, up)),
        (5, end_x, pl.ds(TOP - 1, 1), 1, pl.ds(end_z - 1, 1), (right, down)),
        (10, 0, pl.ds(TOP - 1, 1), width_x, pl.ds(end_z - 1, 1), (left, down)),
        (11, 0, pl.ds(end_z, 1), width_x, pl.ds(TOP, 1), (left, up)),
    ]
    late_x, early_x = pl.ds(2, width_x - 1), pl.ds(1, width_x - 1)
    faces_z = [
        (pl.ds(12, 3), all_x, pl.ds(end_z, 1), all_x, pl.ds(TOP, 1), (gx, up)),
        (4, late_x, pl.ds(end_z, 1), late_x, pl.ds(TOP, 1), (gx, up)),
        (11, early_x, pl.ds(end_z, 1), early_x, pl.ds(TOP, 1), (gx, up)),
        (pl.ds(16, 3), all_x, pl.ds(TOP - 1, 1), all_x, pl.ds(end_z - 1, 1), (gx, down)),
        (10, early_x, pl.ds(TOP - 1, 1), early_x, pl.ds(end_z - 1, 1), (gx, down)),
        (5, late_x, pl.ds(TOP - 1, 1), late_x, pl.ds(end_z - 1, 1), (gx, down)),
    ]

    faces_h = [
        (3, end_x, all_z, 1, all_z, (right, gz)),
        (9, 0, all_z, width_x, all_z, (left, gz)),
        (15, all_x, pl.ds(end_z, 1), all_x, pl.ds(TOP, 1), (gx, up)),
        (19, all_x, pl.ds(TOP - 1, 1), all_x, pl.ds(end_z - 1, 1), (gx, down)),
    ]

    def halo(t, first, faces):
        copies = []
        for j, face in enumerate(faces):
            if face is None:
                continue
            k, x_from, z_from, x_to, z_to, to = face
            copies.append(
                pltpu.make_async_remote_copy(
                    src_ref=states[t + 1].at[k, x_from, z_from, :],
                    dst_ref=states[t + 1].at[k, x_to, z_to, :],
                    send_sem=halo_ss.at[20 * t + first + j],
                    recv_sem=halo_rs.at[20 * t + first + j],
                    device_id=to,
                    device_id_type=MESH,
                )
            )
            copies[-1].start()
        return copies

    def outer_flow(t):
        copies = []
        for x, side in ((width_x - 1, right), (0, left)):
            over(1, x, 1, lambda x: collide_flow(t, x))
            copies += halo(t, 0, [face if face[5][0] is side else None for face in faces_x])
        return copies

    def inner_flow(t):
        over(width_x - 2, 1, 1, lambda x: collide_flow(t, x))
        return halo(t, 10, faces_z)

    def heat(t):
        over(width_x, 0, 1, lambda x: collide_heat(t, x))
        return halo(t, 16, faces_h)

    def landed(copies):
        for copy in copies:
            copy.wait_recv()

    def grow(t, returned):
        high, low = zip(*[halves(returned(s)) for s in range(2)])
        there = product(disp_t[t], jnp.concatenate(high + low, axis=0))
        now = solid[...]
        solid[...] = now + caps[t] * there * (1.0 - now)

    def pack_rows(t, target):
        rows = packed(t)
        target[:, 0, :] = rows[0:n_dev]
        target[:, 1, :] = rows[n_dev : 2 * n_dev]

    def fill_back(t, target):
        rows = gather_mx(t)
        target[:, 0, :] = rows[0:n_dev]
        target[:, 1, :] = rows[n_dev : 2 * n_dev]

    for copy in loads:
        copy.wait()
    outer_moments(0)
    inner_moments(0)
    all_heat_moments(0)
    drags[...] = jnp.zeros(drags.shape, F32)
    rows_here(0, out0_r)
    make_pick(0)
    fill_back(0, back0_s)
    send_rows(1, back0_s, back0_r)
    make_pick_t(0)
    make_facts(0)
    heat_cover(0)
    h0 = heat(0)
    make_spread(0)
    outer_cover(0)
    x0 = outer_flow(0)
    make_pick(1)
    inner_cover(0)
    rows_here(1, back0_r)
    grow(0, lambda s: back0_r[:, s, :])
    pack_rows(1, out1_s)
    send_rows(2, out1_s, out1_r)
    landed(h0)
    all_heat_moments(1)
    fill_back(1, back1_s)
    send_rows(3, back1_s, back1_r)
    z0 = inner_flow(0)
    gather_speed(0)
    make_drag(0)
    make_pick_t(1)
    make_facts(1)
    make_pick(2)
    make_pick_t(2)
    make_facts(2)
    landed(z0)
    inner_moments(1)
    landed(x0)
    outer_moments(1)
    gather_speed(1)

    rows_here(2, out1_r)
    make_spread(1)
    outer_cover(1)
    x1 = outer_flow(1)
    rows_here(3, back1_r)
    grow(1, lambda s: back1_r[:, s, :])
    pack_rows(2, out2_s)
    send_rows(4, out2_s, out2_r)
    heat_cover(1)
    h1 = heat(1)
    inner_cover(1)
    z1 = inner_flow(1)
    make_drag(1)

    landed(h1)
    all_heat_moments(2)
    rows = gather_mx(2)
    back2_s[:, 0, 0:128] = rows[0:n_dev]
    back2_s[:, 0, 128:256] = rows[n_dev : 2 * n_dev]
    landed(z1)
    inner_moments(2)
    landed(x1)
    outer_moments(2)
    gather_speed(2)
    rows_here(4, out2_r)
    make_drag(2)
    back2_s[:, 0, 256:384] = drags[...]
    send_rows(5, back2_s, back2_r)
    make_spread(2)
    outer_cover(2)
    x2 = outer_flow(2)
    heat_cover(2)
    h2 = heat(2)
    inner_cover(2)
    z2 = inner_flow(2)
    rows_here(5, back2_r)
    grow(2, lambda s: back2_r[:, 0, s * 128 : (s + 1) * 128])
    solid_out[...] = solid[...]
    means = back2_r[:, 0, 256:384].T
    total = jnp.zeros((8, grains), F32)
    for t in range(3):
        for s in range(2):
            at = 8 * (2 * t + s)
            high, low = halves(means[at : at + 8, :])
            d = disp[t, s * n_dev : (s + 1) * n_dev, 0:grains]
            total = total + product(high, d) + product(low, d)
    drag_out[...] = total[0:3, :] * DRAG_SCALE

    landed(h2 + z2 + x2)
    for copy in h0 + x0 + z0 + h1 + x1 + z1 + h2 + x2 + z2:
        copy.wait_send()
    sources = (out0_s, back0_s, out1_s, back1_s, out2_s, back2_s)
    for which, source in enumerate(sources):
        rows_sent(which, source)


def deliver(state, solid, drag, flow_out, heat_out, solid_out, drag_out, sem):
    width_x, width_z = flow_out.shape[1], flow_out.shape[2]
    copies = [
        pltpu.make_async_copy(solid, solid_out, sem.at[26]),
        pltpu.make_async_copy(drag, drag_out, sem.at[27]),
    ]
    for k in range(26):
        goal = flow_out.at[k] if k < 19 else heat_out.at[k - 19]
        source = state.at[PLACE[k], pl.ds(1, width_x), pl.ds(TOP, width_z), :]
        copies.append(pltpu.make_async_copy(source, goal, sem.at[k]))
    for copy in copies:
        copy.start()
    for copy in copies:
        copy.wait()


def on_device(sizes, populations, thermal, solid_blocks, centre_dev, centre_col, grain_velocity, capture):
    n_dev = sizes[0] * sizes[1]
    width_x, width_z, width_y = populations.shape[1:]
    grains = solid_blocks.shape[0]
    cells = width_x * width_z
    vmem = pl.BlockSpec(memory_space=pltpu.VMEM)
    state = pltpu.VMEM((26, width_x + 2, width_z + 16, width_y), F32)
    wide = pltpu.VMEM((n_dev, 1, 384), F32)
    plain = pltpu.VMEM((n_dev, 2, 128), F32)
    plane = (width_x, width_z, width_y)
    hbm = pl.BlockSpec(memory_space=pltpu.HBM)
    operands = (
        populations,
        thermal,
        solid_blocks,
        jnp.swapaxes(centre_dev, 1, 2),
        centre_col,
        grain_velocity,
        capture,
    )
    after, solid, drag = pl.pallas_call(
        functools.partial(kernel, sizes),
        out_shape=(
            state,
            pltpu.VMEM(solid_blocks.shape, F32),
            pltpu.VMEM((3, grains), F32),
        ),
        in_specs=[hbm] * 7,
        out_specs=(vmem, vmem, vmem),
        scratch_shapes=[
            state, state, state,
            pltpu.VMEM((3, 1, grains), jnp.int32),
            pltpu.VMEM((3, grains), jnp.int32),
            pltpu.VMEM((3, 3, grains), jnp.int32),
            pltpu.VMEM((3, grains), jnp.int32),
            pltpu.VMEM(plane, F32),
            pltpu.VMEM((3,) + plane, F32),
            pltpu.VMEM((2,) + plane, F32),
            pltpu.VMEM((2 * width_x, width_z, 128), BF16),
            pltpu.VMEM((2 * width_x, width_z, 384), BF16),
            pltpu.VMEM((width_x, width_z, 512), F32),
            pltpu.VMEM(plane, F32),
            pltpu.VMEM((128, grains), F32),
            pltpu.VMEM((3, 2 * n_dev, 2 * cells), BF16),
            pltpu.VMEM((3, cells, 4 * n_dev), BF16),
            pltpu.VMEM((3, 2 * n_dev, 2 * grains), BF16),
            pltpu.VMEM((3, grains, 4 * n_dev), BF16),
            pltpu.VMEM((3, grains, 128), F32),
            pltpu.VMEM((3, 2, 3, n_dev, 128), F32),
            pltpu.VMEM((3, 2, n_dev, 128), F32),
            pltpu.VMEM((4 * n_dev, 512), BF16),
            pltpu.VMEM((4 * n_dev, 128), BF16),
            pltpu.VMEM((grains, 128), F32),
            pltpu.VMEM((n_dev, 128), F32),
            pltpu.VMEM((2 * n_dev, 384), F32),
            wide, wide, plain, plain, plain, plain,
            plain, plain, plain, plain, wide, wide,
            pltpu.SemaphoreType.DMA((31,)),
            pltpu.SemaphoreType.DMA((60,)),
            pltpu.SemaphoreType.DMA((60,)),
            pltpu.SemaphoreType.DMA((6,)),
            pltpu.SemaphoreType.DMA((6,)),
        ],
        compiler_params=pltpu.CompilerParams(
            collective_id=0, has_side_effects=True, vmem_limit_bytes=50 * 1024 * 1024
        ),
    )(*[pltpu.with_memory_space_constraint(given, pltpu.HBM) for given in operands])
    return pl.pallas_call(
        deliver,
        out_shape=(
            jax.ShapeDtypeStruct(populations.shape, F32),
            jax.ShapeDtypeStruct(thermal.shape, F32),
            jax.ShapeDtypeStruct(solid_blocks.shape, F32),
            jax.ShapeDtypeStruct((3, grains), F32),
        ),
        in_specs=[vmem] * 3,
        out_specs=[hbm] * 4,
        scratch_shapes=[pltpu.SemaphoreType.DMA((28,))],
        compiler_params=pltpu.CompilerParams(vmem_limit_bytes=1024 * 1024),
    )(*[pltpu.with_memory_space_constraint(made, pltpu.VMEM) for made in (after, solid, drag)])


def solution(mesh):
    sizes = (mesh.shape["gx"], mesh.shape["gz"])
    placed = (
        P(None, "gx", "gz", None),
        P(None, "gx", "gz", None),
        P(("gx", "gz"), None),
        P(None, ("gx", "gz"), None),
        P(None, ("gx", "gz")),
        P(None, None, ("gx", "gz")),
        P(None, ("gx", "gz")),
    )
    return jax.shard_map(
        functools.partial(on_device, sizes),
        mesh=mesh,
        in_specs=placed,
        out_specs=(
            P(None, "gx", "gz", None),
            P(None, "gx", "gz", None),
            P(("gx", "gz"), None),
            P(None, ("gx", "gz")),
        ),
        check_vma=False,
    )
```
